128 devices in a mesh: band: 16 (over x, y_hi, core), lon: 8 (over y_lo, z).
Axes of the slice: x: 4, y: 4 (y_hi: 2, y_lo: 2; y = y_hi * 2 + y_lo), z: 4, core: 2. Of those that a mesh axis runs over, the one named last changes fastest.
Arguments:
- src_tiles: bfloat16 [6, 65536, 128], P(None, ('band', 'lon')), may hold values from -6 to 6
- ent_tile: int32 [32768], P(('band', 'lon')), may hold values from 0 to 65535, as said below
- ent_block: int32 [32768], P(('band', 'lon')), may hold values from 0 to 16383, as said below
- ent_weight: bfloat16 [32768, 128, 128], P(('band', 'lon')), may hold values from 0 to 0.125
- live_count: int32 [128], P(('band', 'lon')), may hold values from 128 to 256, as said below
Outputs:
- remapped: bfloat16 [6, 256, 8192], P(None, 'band', 'lon')
- smoothed: float32 [256, 8192], P('band', 'lon')
The draws below stay inside these ranges and needn't reach their ends.
Inputs may be any that keep to these rules, and one draw needn't show every extreme that they name: `ent_tile`: A slot of device d = b * 8 + l names a tile (b2 * 8 + l) * 512 + t of the same lon index l; of one device's 256 slots exactly 16 name tiles of each band index b2. `ent_block`: A slot of a device names a target block held by that device. `live_count`: devices of band index 0 and 15 have all slots live.
All inputs are finite; a program needn't handle non-finite values.
Results may differ from the reference program's by a relative error of at most 0.0028.
Values may be sent and summed in bfloat16 or wider, within the bound.
No kernel may reach another device: no remote copies, remote signals or barrier semaphores. Data moves between devices by JAX's collectives and lax.ppermute only.
A program may use at most 128 MiB of HBM per device.

```python
import jax
import jax.numpy as jnp
from jax import lax

CH = 6
TPIX = 128
BW = 128
R_DEV = 16
C_DEV = 1024
TILE_DEV = 512
ENT_DEV = 256
NLAT = 256
NLON = 8192
NTILES = 65536
NENT = 32768
N_BAND = 16
N_LON = 8


def draw_ent_tile(key, part):
    ndevices = N_BAND * N_LON
    lon_of = jnp.arange(ndevices, dtype=jnp.int32) % N_LON
    base_owner = jnp.repeat(jnp.arange(N_BAND, dtype=jnp.int32), ENT_DEV // N_BAND)
    subkeys = jax.random.split(jax.random.fold_in(key, 11), ndevices)
    owners = jax.vmap(lambda subkey: jax.random.permutation(subkey, base_owner))(subkeys)
    tile_local = jax.random.randint(jax.random.fold_in(key, 12), (ndevices, ENT_DEV), 0, TILE_DEV)
    global_tile = (owners * N_LON + lon_of[:, None]) * TILE_DEV + tile_local
    return global_tile.reshape(-1).astype(jnp.int32)


def draw_ent_block(key, part):
    ndevices = N_BAND * N_LON
    device = jnp.arange(ndevices, dtype=jnp.int32)
    band_of = device // N_LON
    lon_of = device % N_LON
    blocks_row = C_DEV // BW
    row_pick = jax.random.randint(jax.random.fold_in(key, 21), (ndevices, ENT_DEV), 0, R_DEV)
    column_pick = jax.random.randint(jax.random.fold_in(key, 22), (ndevices, ENT_DEV), 0, blocks_row)
    row_index = band_of[:, None] * R_DEV + row_pick
    column_index = lon_of[:, None] * blocks_row + column_pick
    block_id = row_index * (blocks_row * N_LON) + column_index
    return block_id.reshape(-1).astype(jnp.int32)


def draw_live_count(key, part):
    ndevices = N_BAND * N_LON
    band_of = jnp.arange(ndevices, dtype=jnp.int32) // N_LON
    inner = ENT_DEV // 2 + jax.random.randint(jax.random.fold_in(key, 31), (ndevices,), 0, ENT_DEV // 4 + 1)
    polar = (band_of == 0) | (band_of == N_BAND - 1)
    return jnp.where(polar, ENT_DEV, inner).astype(jnp.int32)


def level_of(rng, dims, shards, smallest, largest):
    factor_of = 1.0
    for dim, blocks in shards:
        draws = jax.random.uniform(jax.random.fold_in(jax.random.fold_in(rng, 6), dim), (blocks,), jnp.float32, smallest / len(shards), largest / len(shards))
        factor_of = factor_of * jnp.repeat(jnp.exp(draws), dims[dim] // blocks).reshape((-1,) + (1,) * (len(dims) - 1 - dim))
    return factor_of


def centred(stream_key, extent, width, bound, cuts=(), held_as=jnp.bfloat16):
    values = width * jax.random.normal(stream_key, extent, jnp.float32)
    if cuts:
        values = values * level_of(stream_key, extent, cuts, -0.22, 0.18)
    return jnp.clip(values, -bound, bound).astype(held_as)


def setup_inputs(seed: int = 0) -> dict:
    key_of = jax.random.split(jax.random.key(seed), 6)
    return {
        "src_tiles": centred(key_of[0], (CH, NTILES, TPIX), 1.0, 6.0, ((1, 128),)),
        "ent_tile": draw_ent_tile(jax.random.fold_in(key_of[5], 71), 0),
        "ent_block": draw_ent_block(jax.random.fold_in(key_of[5], 71), 0),
        "ent_weight": jnp.clip(0.125 * jax.random.uniform(key_of[3], (NENT, TPIX, BW), jnp.float32) ** level_of(key_of[3], (NENT, TPIX, BW), ((0, 128),), -0.2, 0.2), 0.0, 0.125).astype(jnp.bfloat16),
        "live_count": draw_live_count(jax.random.fold_in(key_of[5], 71), 0),
    }


lat_start = 0.5


def ninepoint_filter(field):
    padded = jnp.pad(field, ((1, 1), (0, 0)))
    north = padded[2:]
    south = padded[:-2]
    sides = north + south + jnp.roll(field, -1, axis=1) + jnp.roll(field, 1, axis=1)
    corners = jnp.roll(north, -1, axis=1) + jnp.roll(north, 1, axis=1) + jnp.roll(south, -1, axis=1) + jnp.roll(south, 1, axis=1)
    return (4.0 * field + 2.0 * sides + corners) / 16.0


def reference(src_tiles, ent_tile, ent_block, ent_weight, live_count):
    ndevices = N_BAND * N_LON

    def per_device(totals, device):
        first = (device * ENT_DEV).astype(jnp.int32)
        tile_ids = lax.dynamic_slice_in_dim(ent_tile, first, ENT_DEV)
        block_ids = lax.dynamic_slice_in_dim(ent_block, first, ENT_DEV)
        weights = lax.dynamic_slice_in_dim(ent_weight, first, ENT_DEV, 0)
        live_mask = jnp.arange(ENT_DEV, dtype=jnp.int32) < live_count[device]
        picked = jnp.take(src_tiles, tile_ids, axis=1).astype(jnp.float32)
        summand = jnp.einsum("cek,ekn->cen", picked, weights.astype(jnp.float32))
        summand = jnp.where(live_mask[None, :, None], summand, 0.0)
        return totals.at[:, block_ids, :].add(summand), None

    totals = jnp.zeros((CH, NLAT * NLON // BW, BW), jnp.float32)
    totals, discarded_value = lax.scan(per_device, totals, jnp.arange(ndevices, dtype=jnp.int32))
    remapped = totals.reshape(CH, NLAT, NLON).astype(jnp.bfloat16)
    east_wind = remapped[2].astype(jnp.float32)
    north_wind = remapped[3].astype(jnp.float32)
    grid_step = 2.0 * jnp.pi / NLON
    latitude = lat_start + (jnp.arange(NLAT, dtype=jnp.float32) + 0.5) * grid_step
    cosine = jnp.cos(latitude)[:, None]
    wind_cos = jnp.pad(east_wind * cosine, ((1, 1), (0, 0)))
    vort = 0.5 * ((jnp.roll(north_wind, -1, axis=1) - jnp.roll(north_wind, 1, axis=1)) - (wind_cos[2:] - wind_cos[:-2])) / cosine
    smoothed = ninepoint_filter(ninepoint_filter(vort))
    return remapped, smoothed
```

```python
import functools
import math

import jax
import jax.numpy as jnp
from jax import lax
from jax.experimental import pallas as pl
from jax.experimental.pallas import tpu as pltpu
from jax.sharding import PartitionSpec as P

BW = 128
R_DEV = 16
C_DEV = 1024
BLK_ROW = C_DEV // BW
LAT_START = 0.5
HALO = 3
EXT = 24
CHUNK = 32

VM = pl.BlockSpec(memory_space=pltpu.VMEM)
SM = pl.BlockSpec(memory_space=pltpu.SMEM)


def dot(a, b):
    return jnp.dot(a, b, preferred_element_type=jnp.float32)


def dot_nt(a, b):
    return lax.dot_general(a, b, (((1,), (1,)), ((), ())), preferred_element_type=jnp.float32)


def iota(shape, dim):
    return lax.broadcasted_iota(jnp.int32, shape, dim)


def as_bf16(flags):
    return flags.astype(jnp.float32).astype(jnp.bfloat16)


def route_kernel(per_band, tiles_held, tile_ref, req_ref, pos_ref):
    tile = tile_ref[...]
    slots = tile.shape[1]
    bands = req_ref.shape[0]
    owner = tile // per_band
    local = tile % tiles_held
    hit = owner == iota((bands, slots), 0)
    before = as_bf16(iota((slots, slots), 0) < iota((slots, slots), 1))
    earlier = dot(as_bf16(hit), before)
    rank = jnp.sum(jnp.where(hit, earlier, 0.0), axis=0, keepdims=True).astype(jnp.int32)
    place = as_bf16(rank == iota((128, slots), 0))
    high = jnp.where(hit, (local // 16).astype(jnp.float32), 0.0).astype(jnp.bfloat16)
    low = jnp.where(hit, (local % 16).astype(jnp.float32), 0.0).astype(jnp.bfloat16)
    req_ref[...] = (dot_nt(high, place) * 16.0 + dot_nt(low, place)).astype(jnp.int32)
    pos_ref[...] = jnp.broadcast_to(owner * (slots // bands) + rank, (8, slots))


def pick_kernel(req_ref, src_ref, send_ref):
    channels, tiles, _ = src_ref.shape
    bands = req_ref.shape[0]
    each = send_ref.shape[1] // channels
    asked = jnp.transpose(req_ref[...].astype(jnp.float32)).astype(jnp.int32)
    cell = iota((each, tiles), 1)
    onehot = jnp.concatenate([as_bf16(asked[:each, d : d + 1] == cell) for d in range(bands)], axis=0)
    for c in range(channels):
        got = dot(onehot, src_ref[c]).astype(jnp.bfloat16)
        send_ref[:, c * each : (c + 1) * each, :] = got.reshape(bands, each, 128)


def remap_kernel(
    row_stride, place_ref, live_ref, recv_ref, pos_ref, block_ref, weight_hbm,
    out_ref, wind_ref, a_ref, b_ref, weight, xs, term, sems,
):
    bands = recv_ref.shape[0]
    slots = weight.shape[0]
    channels = out_ref.shape[0]
    each = slots // bands
    copies = []
    for g in range(slots // CHUNK):
        part = pl.ds(g * CHUNK, CHUNK)
        copies.append(pltpu.make_async_copy(weight_hbm.at[part], weight.at[part], sems.at[g]))
        copies[-1].start()
    where_from = jnp.transpose(pos_ref[...].astype(jnp.float32))[:, :1].astype(jnp.int32)
    perm = as_bf16(where_from == iota((slots, slots), 1))
    for c in range(channels):
        arrived = recv_ref[:, c * each : (c + 1) * each, :].reshape(slots, 128)
        xs[pl.ds(c, slots, stride=8), :] = dot(perm, arrived)
    upper = iota((16, 128), 0) < 8
    for g in range(slots // CHUNK):
        copies[g].wait()
        for s in range(g * CHUNK, (g + 1) * CHUNK, 2):
            x = xs[s * 8 : s * 8 + 16, :]
            pair = jnp.concatenate([jnp.where(upper, x, 0.0), jnp.where(upper, 0.0, x)], axis=1)
            term[s * 8 : s * 8 + 16, :] = dot(pair.astype(jnp.bfloat16), weight[s : s + 2].reshape(256, 128))
    block = block_ref[...]
    target = (block % BLK_ROW) * R_DEV + (block // row_stride) % R_DEV
    live = iota((1, slots), 1) < live_ref[0]
    chosen = as_bf16((target == iota((BLK_ROW * R_DEV, slots), 0)) & live)
    winds = []
    for c in (2, 3, 0, 1, 4, 5):
        rest = term[pl.ds(c, slots, stride=8), :]
        total = None
        for _ in range(3):
            part = rest.astype(jnp.bfloat16)
            rest = rest - part.astype(jnp.float32)
            share = dot(chosen, part)
            total = share if total is None else total + share
        field = jnp.concatenate([total[j * R_DEV : (j + 1) * R_DEV] for j in range(BLK_ROW)], axis=1)
        rounded = field.astype(jnp.bfloat16)
        out_ref[c] = rounded
        if c in (2, 3):
            wind_ref[c - 2] = rounded
            winds.append(rounded.astype(jnp.float32))
        if c == 3:
            pad = jnp.zeros((8 - 2 * HALO, C_DEV), jnp.float32)
            first = jnp.concatenate([w[:HALO] for w in winds] + [pad], axis=0)
            last = jnp.concatenate([w[R_DEV - HALO :] for w in winds] + [pad], axis=0)
            odd = place_ref[0] > 0
            a_ref[...] = jnp.where(odd, first, last).astype(jnp.bfloat16)
            b_ref[...] = jnp.where(odd, last, first).astype(jnp.bfloat16)


def extend_kernel(place_ref, wind_ref, from_a_ref, from_b_ref, ext_ref, a_ref, b_ref):
    from_a = from_a_ref[...].astype(jnp.float32)
    from_b = from_b_ref[...].astype(jnp.float32)
    odd = place_ref[0] > 0
    above = jnp.where(odd, from_a, from_b)
    below = jnp.where(odd, from_b, from_a)
    pad = jnp.zeros((EXT - R_DEV - 2 * HALO, C_DEV), jnp.float32)
    left, right = [], []
    for w in range(2):
        rows = slice(w * HALO, (w + 1) * HALO)
        full = jnp.concatenate([above[rows], wind_ref[w].astype(jnp.float32), below[rows], pad], axis=0)
        ext_ref[w] = full
        left.append(full[:, :128])
        right.append(full[:, C_DEV - 128 :])
    left = jnp.concatenate(left, axis=0)
    right = jnp.concatenate(right, axis=0)
    odd = place_ref[1] > 0
    a_ref[...] = jnp.where(odd, left, right).astype(jnp.bfloat16)
    b_ref[...] = jnp.where(odd, right, left).astype(jnp.bfloat16)


def smooth(x):
    rows, columns = x.shape
    x = 2.0 * x + (pltpu.roll(x, 1, 0) + pltpu.roll(x, rows - 1, 0))
    x = 2.0 * x + (pltpu.roll(x, 1, 1) + pltpu.roll(x, columns - 1, 1))
    return x * (1.0 / 16.0)


def smooth_kernel(grid_step, all_rows, place_ref, ext_ref, from_a_ref, from_b_ref, out_ref):
    from_a = from_a_ref[...].astype(jnp.float32)
    from_b = from_b_ref[...].astype(jnp.float32)
    odd = place_ref[1] > 0
    left = jnp.where(odd, from_a, from_b)
    right = jnp.where(odd, from_b, from_a)
    east, north = (
        jnp.concatenate([left[w * EXT : (w + 1) * EXT], ext_ref[w], right[w * EXT : (w + 1) * EXT]], axis=1)
        for w in range(2)
    )
    rows, columns = east.shape
    row = place_ref[2] - HALO + iota((rows, 128), 0)
    inside = jnp.tile((row >= 0) & (row < all_rows), (1, columns // 128))
    cosine = jnp.tile(jnp.cos(LAT_START + (row.astype(jnp.float32) + 0.5) * grid_step), (1, columns // 128))
    scaled = east * cosine
    along = pltpu.roll(north, columns - 1, 1) - pltpu.roll(north, 1, 1)
    across = pltpu.roll(scaled, rows - 1, 0) - pltpu.roll(scaled, 1, 0)
    field = jnp.where(inside, 0.5 * (along - across) / cosine, 0.0)
    field = jnp.where(inside, smooth(field), 0.0)
    field = smooth(field)
    out_ref[...] = field[HALO : HALO + R_DEV, 128 : 128 + C_DEV]


def call(kernel, outs, ins, scratch=(), vmem=None):
    return pl.pallas_call(
        kernel,
        out_shape=outs,
        in_specs=ins,
        out_specs=jax.tree.map(lambda _: VM, outs),
        scratch_shapes=scratch,
        compiler_params=pltpu.CompilerParams(vmem_limit_bytes=vmem),
    )


def on_device(src_tiles, ent_tile, ent_block, ent_weight, live_count):
    bands, lons = lax.axis_size("band"), lax.axis_size("lon")
    band, lon = lax.axis_index("band"), lax.axis_index("lon")
    channels, tiles, pixels = src_tiles.shape
    slots = ent_tile.shape[0]
    each = slots // bands
    shape = jax.ShapeDtypeStruct
    bf16, f32, i32 = jnp.bfloat16, jnp.float32, jnp.int32
    place = jnp.stack([band % 2, lon % 2, band * R_DEV]).astype(i32)

    req, pos = call(
        functools.partial(route_kernel, lons * tiles, tiles),
        (shape((bands, 128), i32), shape((8, slots), i32)),
        [VM],
    )(ent_tile.reshape(1, slots))
    asked = lax.all_to_all(req, "band", 0, 0, tiled=True)
    send = call(pick_kernel, shape((bands, channels * each, pixels), bf16), [VM, VM], vmem=16 << 20)(asked, src_tiles)
    recv = lax.all_to_all(send, "band", 0, 0, tiled=True)

    rows = shape((8, C_DEV), bf16)
    remapped, wind, to_a, to_b = call(
        functools.partial(remap_kernel, BLK_ROW * lons),
        (shape((channels, R_DEV, C_DEV), bf16), shape((2, R_DEV, C_DEV), bf16), rows, rows),
        [SM, SM, VM, VM, VM, pl.BlockSpec(memory_space=pl.ANY)],
        [
            pltpu.VMEM((slots, pixels, BW), bf16),
            pltpu.VMEM((slots * 8, pixels), f32),
            pltpu.VMEM((slots * 8, BW), f32),
            pltpu.SemaphoreType.DMA((slots // CHUNK,)),
        ],
        vmem=32 << 20,
    )(place, live_count, recv, pos, ent_block.reshape(1, slots), ent_weight)

    pairs_a = lambda size: [(i, i ^ 1) for i in range(size)]
    pairs_b = [(i, i + 1 if i % 2 else i - 1) for i in range(1, bands - 1)]
    ring_b = [(i, (i + 1 if i % 2 else i - 1) % lons) for i in range(lons)]
    from_b = lax.ppermute(to_b, "band", pairs_b)
    from_a = lax.ppermute(to_a, "band", pairs_a(bands))
    edge = shape((2 * EXT, 128), bf16)
    ext, to_a, to_b = call(extend_kernel, (shape((2, EXT, C_DEV), f32), edge, edge), [SM, VM, VM, VM])(
        place, wind, from_a, from_b
    )
    from_b = lax.ppermute(to_b, "lon", ring_b)
    from_a = lax.ppermute(to_a, "lon", pairs_a(lons))
    smoothed = call(
        functools.partial(smooth_kernel, 2.0 * math.pi / (C_DEV * lons), R_DEV * bands),
        shape((R_DEV, C_DEV), f32),
        [SM, VM, VM, VM],
    )(place, ext, from_a, from_b)
    return remapped, smoothed


def solution(mesh):
    in_specs = (
        P(None, ("band", "lon"), None),
        P(("band", "lon")),
        P(("band", "lon")),
        P(("band", "lon"), None, None),
        P(("band", "lon")),
    )
    out_specs = (P(None, "band", "lon"), P("band", "lon"))
    return jax.shard_map(on_device, mesh=mesh, in_specs=in_specs, out_specs=out_specs, check_vma=False)
```

```python
import functools
import math

import jax
import jax.numpy as jnp
from jax import lax
from jax.experimental import pallas as pl
from jax.experimental.pallas import tpu as pltpu
from jax.sharding import PartitionSpec as P

BW = 128
R_DEV = 16
C_DEV = 1024
BLK_ROW = C_DEV // BW
LAT_START = 0.5
HALO = 3
HELD = 80
CHUNK = 16
EXT = 24

VM = pl.BlockSpec(memory_space=pltpu.VMEM)
SM = pl.BlockSpec(memory_space=pltpu.SMEM)
HB = pl.BlockSpec(memory_space=pltpu.HBM)
ANY = pl.BlockSpec(memory_space=pl.ANY)


def dot(a, b):
    return jnp.dot(a, b, preferred_element_type=jnp.float32)


def dot_nt(a, b):
    return lax.dot_general(a, b, (((1,), (1,)), ((), ())), preferred_element_type=jnp.float32)


def iota(shape, dim):
    return lax.broadcasted_iota(jnp.int32, shape, dim)


def as_bf16(flags):
    return flags.astype(jnp.float32).astype(jnp.bfloat16)


def is_odd(axis):
    return lax.axis_index(axis) % 2 == 1


def first_row():
    return lax.axis_index("band") * R_DEV


def route_kernel(per_band, tiles_held, tile_ref, req_ref, pos_ref):
    tile = tile_ref[...]
    slots = tile.shape[1]
    bands = req_ref.shape[0]
    owner = tile // per_band
    local = tile % tiles_held
    hit = owner == iota((bands, slots), 0)
    before = as_bf16(iota((slots, slots), 0) < iota((slots, slots), 1))
    earlier = dot(as_bf16(hit), before)
    rank = jnp.sum(jnp.where(hit, earlier, 0.0), axis=0, keepdims=True).astype(jnp.int32)
    place = as_bf16(rank == iota((128, slots), 0))
    high = jnp.where(hit, (local // 16).astype(jnp.float32), 0.0).astype(jnp.bfloat16)
    low = jnp.where(hit, (local % 16).astype(jnp.float32), 0.0).astype(jnp.bfloat16)
    req_ref[...] = (dot_nt(high, place) * 16.0 + dot_nt(low, place)).astype(jnp.int32)
    pos_ref[...] = jnp.broadcast_to(owner * (slots // bands) + rank, (8, slots))


def pick_kernel(req_ref, src_ref, send_hbm, picked, sems):
    channels, tiles, _ = src_ref.shape
    _, bands, each, _ = picked.shape
    asked = jnp.transpose(req_ref[...].astype(jnp.float32)).astype(jnp.int32)
    cell = iota((each, tiles), 1)
    onehot = jnp.concatenate([as_bf16(asked[:each, d : d + 1] == cell) for d in range(bands)], axis=0)
    copies = []
    for c in range(channels):
        got = dot(onehot, src_ref[c]).astype(jnp.bfloat16)
        picked[c] = got.reshape(bands, each, 128)
        copies.append(pltpu.make_async_copy(picked.at[c], send_hbm.at[:, pl.ds(c * each, each)], sems.at[c]))
        copies[-1].start()
    for copy in copies:
        copy.wait()


def start_copies(source, target, sems, first=0):
    parts = sems.shape[0]
    size = target.shape[0] // parts
    copies = []
    for g in range(parts):
        part = source.at[pl.ds(first + g * size, size)]
        copies.append(pltpu.make_async_copy(part, target.at[pl.ds(g * size, size)], sems.at[g]))
        copies[-1].start()
    return copies


def stage_kernel(after_ref, source_hbm, held_ref, sems):
    for copy in start_copies(source_hbm, held_ref, sems):
        copy.wait()


def select_kernel(row_stride, grid_step, live_ref, pos_ref, block_ref, perm_ref, chosen_ref, cosine_ref):
    slots = pos_ref.shape[1]
    where_from = jnp.transpose(pos_ref[...].astype(jnp.float32))[:, :1].astype(jnp.int32)
    perm_ref[...] = as_bf16(where_from == iota((slots, slots), 1))
    block = block_ref[...]
    target = (block % BLK_ROW) * R_DEV + (block // row_stride) % R_DEV
    live = iota((1, slots), 1) < live_ref[0]
    chosen_ref[...] = as_bf16((target == iota((BLK_ROW * R_DEV, slots), 0)) & live)
    row = first_row() - HALO + iota(cosine_ref.shape, 0)
    cosine_ref[...] = jnp.cos(LAT_START + (row.astype(jnp.float32) + 0.5) * grid_step)


def add_blocks(chosen, rest):
    total = None
    for _ in range(3):
        part = rest.astype(jnp.bfloat16)
        rest = rest - part.astype(jnp.float32)
        share = dot(chosen, part)
        total = share if total is None else total + share
    field = jnp.concatenate([total[j * R_DEV : (j + 1) * R_DEV] for j in range(BLK_ROW)], axis=1)
    return field.astype(jnp.bfloat16)


def remap_kernel(
    recv_ref, perm_ref, chosen_ref, held_ref, weight_hbm,
    wind_ref, a_ref, b_ref, others_ref, weight, xs, term, sems,
):
    bands = recv_ref.shape[0]
    slots, held = perm_ref.shape[0], held_ref.shape[0]
    channels = 2 + others_ref.shape[0]
    each = slots // bands
    chunk = (slots - held) // sems.shape[0]
    copies = start_copies(weight_hbm, weight, sems, held)
    perm = perm_ref[...]
    for c in range(channels):
        xs[c] = dot(perm, recv_ref[:, c * each : (c + 1) * each, :].reshape(slots, 128))
    row = iota((8 * channels, 128), 0) % 8
    masks = [as_bf16(row == j) for j in range(8)]
    for s in range(0, slots, 8):
        if s >= held and (s - held) % chunk == 0:
            copies[(s - held) // chunk].wait()
        x = jnp.concatenate([xs[c, s : s + 8, :] for c in range(channels)], axis=0).astype(jnp.bfloat16)
        spread = jnp.concatenate([x * mask for mask in masks], axis=1)
        eight = held_ref[s : s + 8] if s < held else weight[s - held : s - held + 8]
        got = dot(spread, eight.reshape(8 * 128, 128))
        for c in range(channels):
            target = term.at[c - 2] if c in (2, 3) else others_ref.at[c if c < 2 else c - 2]
            target[s : s + 8, :] = got[c * 8 : (c + 1) * 8]
    winds = []
    for w in range(2):
        rounded = add_blocks(chosen_ref[...], term[w])
        wind_ref[w] = rounded
        winds.append(rounded.astype(jnp.float32))
    pad = jnp.zeros((8 - 2 * HALO, C_DEV), jnp.float32)
    first = jnp.concatenate([w[:HALO] for w in winds] + [pad], axis=0)
    last = jnp.concatenate([w[R_DEV - HALO :] for w in winds] + [pad], axis=0)
    odd = is_odd("band")
    a_ref[...] = jnp.where(odd, first, last).astype(jnp.bfloat16)
    b_ref[...] = jnp.where(odd, last, first).astype(jnp.bfloat16)


def finish_kernel(chosen_ref, others_ref, wind_ref, out_ref):
    for c in range(out_ref.shape[0]):
        if c in (2, 3):
            out_ref[c] = wind_ref[c - 2]
        else:
            out_ref[c] = add_blocks(chosen_ref[...], others_ref[c if c < 2 else c - 2])


def extend_kernel(after_ref, wind_ref, from_a_ref, from_b_ref, ext_ref, a_ref, b_ref):
    from_a = from_a_ref[...].astype(jnp.float32)
    from_b = from_b_ref[...].astype(jnp.float32)
    odd = is_odd("band")
    above = jnp.where(odd, from_a, from_b)
    below = jnp.where(odd, from_b, from_a)
    pad = jnp.zeros((EXT - R_DEV - 2 * HALO, C_DEV), jnp.float32)
    left, right = [], []
    for w in range(2):
        rows = slice(w * HALO, (w + 1) * HALO)
        full = jnp.concatenate([above[rows], wind_ref[w].astype(jnp.float32), below[rows], pad], axis=0)
        ext_ref[w] = full
        left.append(full[:, :128])
        right.append(full[:, C_DEV - 128 :])
    left = jnp.concatenate(left, axis=0)
    right = jnp.concatenate(right, axis=0)
    odd = is_odd("lon")
    a_ref[...] = jnp.where(odd, left, right).astype(jnp.bfloat16)
    b_ref[...] = jnp.where(odd, right, left).astype(jnp.bfloat16)


def smooth(x):
    rows, columns = x.shape
    x = 2.0 * x + (pltpu.roll(x, 1, 0) + pltpu.roll(x, rows - 1, 0))
    x = 2.0 * x + (pltpu.roll(x, 1, 1) + pltpu.roll(x, columns - 1, 1))
    return x * (1.0 / 16.0)


def smooth_kernel(all_rows, cosine_ref, ext_ref, from_a_ref, from_b_ref, out_ref):
    from_a = from_a_ref[...].astype(jnp.float32)
    from_b = from_b_ref[...].astype(jnp.float32)
    odd = is_odd("lon")
    left = jnp.where(odd, from_a, from_b)
    right = jnp.where(odd, from_b, from_a)
    east, north = (
        jnp.concatenate([left[w * EXT : (w + 1) * EXT], ext_ref[w], right[w * EXT : (w + 1) * EXT]], axis=1)
        for w in range(2)
    )
    rows, columns = east.shape
    row = first_row() - HALO + iota((rows, 128), 0)
    inside = jnp.tile((row >= 0) & (row < all_rows), (1, columns // 128))
    cosine = cosine_ref[...]
    scaled = east * jnp.tile(cosine, (1, columns // 128))
    half = jnp.tile(0.5 / cosine, (1, columns // 128))
    along = pltpu.roll(north, columns - 1, 1) - pltpu.roll(north, 1, 1)
    across = pltpu.roll(scaled, rows - 1, 0) - pltpu.roll(scaled, 1, 0)
    field = jnp.where(inside, (along - across) * half, 0.0)
    field = jnp.where(inside, smooth(field), 0.0)
    field = smooth(field)
    out_ref[...] = field[HALO : HALO + R_DEV, 128 : 128 + C_DEV]


def call(kernel, outs, ins, scratch=(), vmem=2 << 20, cycles=0, out_specs=None):
    return pl.pallas_call(
        kernel,
        out_shape=outs,
        in_specs=ins,
        out_specs=out_specs or jax.tree.map(lambda _: VM, outs),
        scratch_shapes=scratch,
        compiler_params=pltpu.CompilerParams(vmem_limit_bytes=vmem),
        cost_estimate=pl.CostEstimate(flops=cycles, bytes_accessed=cycles, transcendentals=0) if cycles else None,
    )


def on_device(src_tiles, ent_tile, ent_block, ent_weight, live_count):
    bands, lons = lax.axis_size("band"), lax.axis_size("lon")
    channels, tiles, pixels = src_tiles.shape
    slots = ent_tile.shape[0]
    each = slots // bands
    shape = jax.ShapeDtypeStruct
    bf16, f32, i32 = jnp.bfloat16, jnp.float32, jnp.int32
    dmas = pltpu.SemaphoreType.DMA
    held = pltpu.with_memory_space_constraint

    req, pos = call(
        functools.partial(route_kernel, lons * tiles, tiles),
        (shape((bands, 128), i32), shape((8, slots), i32)),
        [VM],
    )(ent_tile.reshape(1, slots))
    asked = lax.all_to_all(req, "band", 0, 0, tiled=True)
    tiles_held = call(
        stage_kernel, pltpu.VMEM(src_tiles.shape, bf16), [ANY, HB], [dmas((channels,))], cycles=2 * src_tiles.size
    )(req, held(src_tiles, pltpu.HBM))
    perm, chosen, cosine = call(
        functools.partial(select_kernel, BLK_ROW * lons, 2.0 * math.pi / (C_DEV * lons)),
        (shape((slots, slots), bf16), shape((BLK_ROW * R_DEV, slots), bf16), shape((EXT, 128), f32)),
        [SM, VM, VM],
        cycles=slots * slots * 8,
    )(live_count, pos, ent_block.reshape(1, slots))
    send = call(
        pick_kernel,
        pltpu.HBM((bands, channels * each, pixels), bf16),
        [VM, VM],
        [pltpu.VMEM((channels, bands, each, pixels), bf16), dmas((channels,))],
        out_specs=HB,
    )(asked, held(tiles_held, pltpu.VMEM))
    recv = lax.all_to_all(send, "band", 0, 0, tiled=True)
    weight_held = call(
        stage_kernel, pltpu.VMEM((HELD, pixels, BW), bf16), [ANY, HB], [dmas((4,))], cycles=2 * HELD * pixels * BW
    )(held(send, pltpu.HBM), held(ent_weight, pltpu.HBM))

    rows = shape((8, C_DEV), bf16)
    wind, to_a, to_b, others = call(
        remap_kernel,
        (shape((2, R_DEV, C_DEV), bf16), rows, rows, shape((channels - 2, slots, BW), f32)),
        [VM, VM, VM, VM, HB],
        [
            pltpu.VMEM((slots - HELD, pixels, BW), bf16),
            pltpu.VMEM((channels, slots, pixels), f32),
            pltpu.VMEM((2, slots, BW), f32),
            dmas(((slots - HELD) // CHUNK,)),
        ],
        vmem=16 << 20,
    )(recv, perm, chosen, held(weight_held, pltpu.VMEM), held(ent_weight, pltpu.HBM))
    remapped = call(
        finish_kernel, shape((channels, R_DEV, C_DEV), bf16), [VM, VM, VM], cycles=slots * slots * 16
    )(chosen, others, wind)

    pairs_a = lambda size: [(i, i ^ 1) for i in range(size)]
    pairs_b = [(i, i + 1 if i % 2 else i - 1) for i in range(1, bands - 1)]
    ring_b = [(i, (i + 1 if i % 2 else i - 1) % lons) for i in range(lons)]
    from_a = lax.ppermute(to_a, "band", pairs_a(bands))
    from_b = lax.ppermute(to_b, "band", pairs_b)
    edge = shape((2 * EXT, 128), bf16)
    ext, to_a, to_b = call(extend_kernel, (shape((2, EXT, C_DEV), f32), edge, edge), [ANY, VM, VM, VM])(
        held(remapped, pltpu.HBM), wind, from_a, from_b
    )
    from_a = lax.ppermute(to_a, "lon", pairs_a(lons))
    from_b = lax.ppermute(to_b, "lon", ring_b)
    smoothed = call(
        functools.partial(smooth_kernel, R_DEV * bands),
        shape((R_DEV, C_DEV), f32),
        [VM, VM, VM, VM],
    )(cosine, ext, from_a, from_b)
    return remapped, smoothed


def solution(mesh):
    in_specs = (
        P(None, ("band", "lon"), None),
        P(("band", "lon")),
        P(("band", "lon")),
        P(("band", "lon"), None, None),
        P(("band", "lon")),
    )
    out_specs = (P(None, "band", "lon"), P("band", "lon"))
    return jax.shard_map(on_device, mesh=mesh, in_specs=in_specs, out_specs=out_specs, check_vma=False)
```

```python
import functools
import math

import jax
import jax.numpy as jnp
from jax import lax
from jax.experimental import pallas as pl
from jax.experimental.pallas import tpu as pltpu
from jax.sharding import PartitionSpec as P

BW = 128
R_DEV = 16
C_DEV = 1024
BLK_ROW = C_DEV // BW
LAT_START = 0.5
HALO = 3
RIM = 8
HELD = 88
CHUNK = 24
EXT = 24

VM = pl.BlockSpec(memory_space=pltpu.VMEM)
SM = pl.BlockSpec(memory_space=pltpu.SMEM)
HB = pl.BlockSpec(memory_space=pltpu.HBM)
ANY = pl.BlockSpec(memory_space=pl.ANY)


def dot(a, b):
    return jnp.dot(a, b, preferred_element_type=jnp.float32)


def dot_nt(a, b):
    return lax.dot_general(a, b, (((1,), (1,)), ((), ())), preferred_element_type=jnp.float32)


def iota(shape, dim):
    return lax.broadcasted_iota(jnp.int32, shape, dim)


def as_bf16(flags):
    return flags.astype(jnp.float32).astype(jnp.bfloat16)


def is_odd(axis):
    return lax.axis_index(axis) % 2 == 1


def first_row():
    return lax.axis_index("band") * R_DEV


def route_kernel(per_band, tiles_held, tile_ref, req_ref, pos_ref):
    tile = tile_ref[...]
    slots = tile.shape[1]
    bands = req_ref.shape[0]
    owner = tile // per_band
    local = tile % tiles_held
    hit = owner == iota((bands, slots), 0)
    before = as_bf16(iota((slots, slots), 0) < iota((slots, slots), 1))
    earlier = dot(as_bf16(hit), before)
    rank = jnp.sum(jnp.where(hit, earlier, 0.0), axis=0, keepdims=True).astype(jnp.int32)
    place = as_bf16(rank == iota((128, slots), 0))
    high = jnp.where(hit, (local // 16).astype(jnp.float32), 0.0).astype(jnp.bfloat16)
    low = jnp.where(hit, (local % 16).astype(jnp.float32), 0.0).astype(jnp.bfloat16)
    req_ref[...] = (dot_nt(high, place) * 16.0 + dot_nt(low, place)).astype(jnp.int32)
    pos_ref[...] = jnp.broadcast_to(owner * (slots // bands) + rank, (8, slots))


def pick_kernel(req_ref, src_ref, send_hbm, picked, sems):
    channels, tiles, _ = src_ref.shape
    _, bands, each, _ = picked.shape
    asked = jnp.transpose(req_ref[...].astype(jnp.float32)).astype(jnp.int32)
    cell = iota((each, tiles), 1)
    onehot = jnp.concatenate([as_bf16(asked[:each, d : d + 1] == cell) for d in range(bands)], axis=0)
    copies = []
    for c in range(channels):
        got = dot(onehot, src_ref[c]).astype(jnp.bfloat16)
        picked[c] = got.reshape(bands, each, 128)
        copies.append(pltpu.make_async_copy(picked.at[c], send_hbm.at[:, pl.ds(c * each, each)], sems.at[c]))
        copies[-1].start()
    for copy in copies:
        copy.wait()


def stage_kernel(after_ref, source_hbm, held_ref, sems):
    copies = [pltpu.make_async_copy(source_hbm.at[c], held_ref.at[c], sems.at[c]) for c in range(sems.shape[0])]
    for copy in copies:
        copy.start()
    for copy in copies:
        copy.wait()


def fetch_weights(order_ref, weight_hbm, target, sem, first, count, offset):
    for i in range(count):
        slot = order_ref[0, first + i]
        pltpu.make_async_copy(weight_hbm.at[slot], target.at[offset + i], sem).start()


def await_weights(weight_hbm, target, sem, count, offset):
    pltpu.make_async_copy(weight_hbm.at[pl.ds(0, count)], target.at[pl.ds(offset, count)], sem).wait()


def hold_kernel(order_ref, after_ref, weight_hbm, held_ref, sems):
    for g in range(sems.shape[0]):
        fetch_weights(order_ref, weight_hbm, held_ref, sems.at[g], g * 8, 8, g * 8)
    for g in range(sems.shape[0]):
        await_weights(weight_hbm, held_ref, sems.at[g], 8, g * 8)


def select_kernel(
    row_stride, grid_step, live_ref, pos_ref, block_ref,
    perm_ref, chosen_ref, rim_ref, order_smem, cosine_ref, order_ref, sem,
):
    slots = pos_ref.shape[1]
    block = block_ref[...]
    row, column = (block // row_stride) % R_DEV, block % BLK_ROW
    lane = iota((1, slots), 1)
    live = lane < live_ref[0]
    at_rim = (row < HALO) | (row >= R_DEV - HALO)
    kind = jnp.where(live, jnp.where(at_rim, 0, 1), 2)
    kinds = iota((8, slots), 0)
    hit = kind == kinds
    earlier = dot(as_bf16(hit), as_bf16(iota((slots, slots), 0) < iota((slots, slots), 1)))
    n_rim = jnp.sum(jnp.where(kind == 0, 1.0, 0.0), axis=1, keepdims=True)
    n_live = jnp.sum(jnp.where(kind < 2, 1.0, 0.0), axis=1, keepdims=True)
    start = jnp.where(kinds == 1, n_rim, jnp.where(kinds == 2, n_live, 0.0))
    place = jnp.sum(jnp.where(hit, earlier + start, 0.0), axis=0, keepdims=True).astype(jnp.int32)
    move = as_bf16(place == iota((slots, slots), 0))
    where_from = dot_nt(move, pos_ref[...].astype(jnp.float32).astype(jnp.bfloat16))[:, :1].astype(jnp.int32)
    perm_ref[...] = as_bf16(where_from == iota((slots, slots), 1))
    target = column * R_DEV + row
    rim_target = jnp.where(at_rim, column * RIM + jnp.where(row < HALO, row, row - (R_DEV - 2 * HALO)), 255)
    facts = [lane, target, live.astype(jnp.int32), rim_target]
    facts = jnp.concatenate([f.astype(jnp.float32) for f in facts + [lane] * 4], axis=0).astype(jnp.bfloat16)
    moved = dot_nt(facts, move).astype(jnp.int32)
    used = moved[2:3] > 0
    chosen_ref[...] = as_bf16((moved[1:2] == iota((BLK_ROW * R_DEV, slots), 0)) & used)
    rim_ref[...] = as_bf16((moved[3:4] == iota((BLK_ROW * RIM, slots), 0)) & used)
    counts = [jnp.broadcast_to(n.astype(jnp.int32), (1, slots)) for n in (n_rim, n_live)]
    order_ref[...] = jnp.concatenate([moved[:1]] + counts + [moved[:1]] * 5, axis=0)
    copy = pltpu.make_async_copy(order_ref, order_smem, sem)
    copy.start()
    row = first_row() - HALO + iota(cosine_ref.shape, 0)
    cosine_ref[...] = jnp.cos(LAT_START + (row.astype(jnp.float32) + 0.5) * grid_step)
    copy.wait()


def add_blocks(chosen, rest):
    total = None
    for _ in range(3):
        part = rest.astype(jnp.bfloat16)
        rest = rest - part.astype(jnp.float32)
        share = dot(chosen, part)
        total = share if total is None else total + share
    rows = chosen.shape[0] // BLK_ROW
    field = jnp.concatenate([total[j * rows : (j + 1) * rows] for j in range(BLK_ROW)], axis=1)
    return field.astype(jnp.bfloat16)


def order_tiles(xs, perm_ref, recv_ref, first, count):
    slots = perm_ref.shape[0]
    each = slots // recv_ref.shape[0]
    for c in range(xs.shape[0]):
        xs[c, first : first + count] = dot(
            perm_ref[first : first + count], recv_ref[:, c * each : (c + 1) * each, :].reshape(slots, 128)
        )


def multiply(xs, eight, terms, first, count):
    channels = xs.shape[0]
    row = iota((8 * channels, 128), 0) % 8
    masks = [as_bf16(row == j) for j in range(8)]
    for g in range(0, count, 8):
        rows = pl.ds(first + g, 8)
        x = jnp.concatenate([xs[c, rows, :] for c in range(channels)], axis=0).astype(jnp.bfloat16)
        spread = jnp.concatenate([x * mask for mask in masks], axis=1)
        got = dot(spread, eight(g))
        for c in range(channels):
            terms[c][rows, :] = got[c * 8 : (c + 1) * 8]


def chunks_of(slots, count):
    return jnp.clip((count - HELD + CHUNK - 1) // CHUNK, 0, (slots - HELD) // CHUNK)


def chunk_steps(order, weight_hbm, weight, xs, terms, sems):
    def fetch(k, carry):
        fetch_weights(order, weight_hbm, weight, sems.at[k], HELD + k * CHUNK, CHUNK, k * CHUNK)
        return carry

    def step(k, carry):
        await_weights(weight_hbm, weight, sems.at[k], CHUNK, k * CHUNK)
        eight = lambda g: weight[pl.ds(k * CHUNK + g, 8)].reshape(8 * 128, 128)
        multiply(xs, eight, terms, pl.multiple_of(HELD + k * CHUNK, 8), CHUNK)
        return carry

    return fetch, step


def rim_kernel(
    order, recv_ref, perm_ref, rim_ref, held_ref, weight_hbm, first_ref, b_ref, term_ref,
    weight, xs, sems,
):
    channels, slots, _ = term_ref.shape
    terms = [term_ref.at[c] for c in range(channels)]
    half = slots // 2
    chunks = chunks_of(slots, order[1, 0])

    fetch, step = chunk_steps(order, weight_hbm, weight, xs, terms, sems)
    lax.fori_loop(0, chunks, fetch, 0)
    order_tiles(xs, perm_ref, recv_ref, 0, half)

    @pl.when(HELD + chunks * CHUNK > half)
    def _():
        order_tiles(xs, perm_ref, recv_ref, half, half)

    for term in terms:
        term[HELD:slots, :] = jnp.zeros((slots - HELD, 128), jnp.float32)
    multiply(xs, lambda g: held_ref[g : g + 8].reshape(8 * 128, 128), terms, 0, HELD)
    lax.fori_loop(0, chunks, step, 0)
    winds = [add_blocks(rim_ref[...], term_ref[c]).astype(jnp.float32) for c in (2, 3)]
    pad = jnp.zeros((8 - 2 * HALO, C_DEV), jnp.float32)
    first = jnp.concatenate([w[:HALO] for w in winds] + [pad], axis=0)
    last = jnp.concatenate([w[HALO : 2 * HALO] for w in winds] + [pad], axis=0)
    odd = is_odd("band")
    first_ref[...] = jnp.where(odd, first, last).astype(jnp.bfloat16)
    b_ref[...] = jnp.where(odd, last, first).astype(jnp.bfloat16)


def rest_kernel(
    after_ref, order, recv_ref, perm_ref, chosen_ref, term_ref, weight_hbm,
    wind_ref, others_ref, weight, xs, term, sems,
):
    channels, slots, _ = term_ref.shape
    terms = [term.at[c - 2] if c in (2, 3) else others_ref.at[c if c < 2 else c - 2] for c in range(channels)]
    first, last = chunks_of(slots, order[1, 0]), chunks_of(slots, order[2, 0])
    fetch, step = chunk_steps(order, weight_hbm, weight, xs, terms, sems)
    lax.fori_loop(first, last, fetch, 0)
    order_tiles(xs, perm_ref, recv_ref, 0, slots)
    for c in range(channels):
        terms[c][...] = term_ref[c]
    lax.fori_loop(first, last, step, 0)
    for w in range(2):
        wind_ref[w] = add_blocks(chosen_ref[...], term[w])


def finish_kernel(after_ref, chosen_ref, others_ref, wind_ref, out_ref):
    for c in range(out_ref.shape[0]):
        if c in (2, 3):
            out_ref[c] = wind_ref[c - 2]
        else:
            out_ref[c] = add_blocks(chosen_ref[...], others_ref[c if c < 2 else c - 2])


def extend_kernel(wind_ref, from_a_ref, from_b_ref, ext_ref, a_ref, b_ref):
    from_a = from_a_ref[...].astype(jnp.float32)
    from_b = from_b_ref[...].astype(jnp.float32)
    odd = is_odd("band")
    above = jnp.where(odd, from_a, from_b)
    below = jnp.where(odd, from_b, from_a)
    pad = jnp.zeros((EXT - R_DEV - 2 * HALO, C_DEV), jnp.float32)
    left, right = [], []
    for w in range(2):
        rows = slice(w * HALO, (w + 1) * HALO)
        full = jnp.concatenate([above[rows], wind_ref[w].astype(jnp.float32), below[rows], pad], axis=0)
        ext_ref[w] = full
        left.append(full[:, :128])
        right.append(full[:, C_DEV - 128 :])
    left = jnp.concatenate(left, axis=0)
    right = jnp.concatenate(right, axis=0)
    odd = is_odd("lon")
    a_ref[...] = jnp.where(odd, left, right).astype(jnp.bfloat16)
    b_ref[...] = jnp.where(odd, right, left).astype(jnp.bfloat16)


def smooth(x):
    rows, columns = x.shape
    x = 2.0 * x + (pltpu.roll(x, 1, 0) + pltpu.roll(x, rows - 1, 0))
    x = 2.0 * x + (pltpu.roll(x, 1, 1) + pltpu.roll(x, columns - 1, 1))
    return x * (1.0 / 16.0)


def smooth_kernel(all_rows, cosine_ref, ext_ref, from_a_ref, from_b_ref, out_ref):
    from_a = from_a_ref[...].astype(jnp.float32)
    from_b = from_b_ref[...].astype(jnp.float32)
    odd = is_odd("lon")
    left = jnp.where(odd, from_a, from_b)
    right = jnp.where(odd, from_b, from_a)
    east, north = (
        jnp.concatenate([left[w * EXT : (w + 1) * EXT], ext_ref[w], right[w * EXT : (w + 1) * EXT]], axis=1)
        for w in range(2)
    )
    rows, columns = east.shape
    row = first_row() - HALO + iota((rows, 128), 0)
    inside = jnp.tile((row >= 0) & (row < all_rows), (1, columns // 128))
    cosine = cosine_ref[...]
    scaled = east * jnp.tile(cosine, (1, columns // 128))
    half = jnp.tile(0.5 / cosine, (1, columns // 128))
    along = pltpu.roll(north, columns - 1, 1) - pltpu.roll(north, 1, 1)
    across = pltpu.roll(scaled, rows - 1, 0) - pltpu.roll(scaled, 1, 0)
    field = jnp.where(inside, (along - across) * half, 0.0)
    field = jnp.where(inside, smooth(field), 0.0)
    field = smooth(field)
    out_ref[...] = field[HALO : HALO + R_DEV, 128 : 128 + C_DEV]


def call(kernel, outs, ins, scratch=(), vmem=2 << 20, cycles=0, out_specs=None):
    return pl.pallas_call(
        kernel,
        out_shape=outs,
        in_specs=ins,
        out_specs=out_specs or jax.tree.map(lambda _: VM, outs),
        scratch_shapes=scratch,
        compiler_params=pltpu.CompilerParams(vmem_limit_bytes=vmem),
        cost_estimate=pl.CostEstimate(flops=cycles, bytes_accessed=cycles, transcendentals=0) if cycles else None,
    )


def on_device(src_tiles, ent_tile, ent_block, ent_weight, live_count):
    bands, lons = lax.axis_size("band"), lax.axis_size("lon")
    channels, tiles, pixels = src_tiles.shape
    slots = ent_tile.shape[0]
    each = slots // bands
    shape = jax.ShapeDtypeStruct
    bf16, f32, i32 = jnp.bfloat16, jnp.float32, jnp.int32
    dmas = pltpu.SemaphoreType.DMA
    held = pltpu.with_memory_space_constraint

    req, pos = call(
        functools.partial(route_kernel, lons * tiles, tiles),
        (shape((bands, 128), i32), shape((8, slots), i32)),
        [VM],
    )(ent_tile.reshape(1, slots))
    asked = lax.all_to_all(req, "band", 0, 0, tiled=True)
    tiles_held = call(
        stage_kernel, pltpu.VMEM(src_tiles.shape, bf16), [ANY, HB], [dmas((channels,))], cycles=2 * src_tiles.size
    )(req, held(src_tiles, pltpu.HBM))
    perm, chosen, rim, order, cosine = call(
        functools.partial(select_kernel, BLK_ROW * lons, 2.0 * math.pi / (C_DEV * lons)),
        (
            shape((slots, slots), bf16),
            shape((BLK_ROW * R_DEV, slots), bf16),
            shape((BLK_ROW * RIM, slots), bf16),
            pltpu.SMEM((8, slots), i32),
            shape((EXT, 128), f32),
        ),
        [SM, VM, VM],
        [pltpu.VMEM((8, slots), i32), dmas],
        out_specs=(VM, VM, VM, SM, VM),
        cycles=slots * slots * 8,
    )(live_count, pos, ent_block.reshape(1, slots))
    order = held(order, pltpu.SMEM)
    weight_hbm = held(ent_weight, pltpu.HBM)
    send = call(
        pick_kernel,
        pltpu.HBM((bands, channels * each, pixels), bf16),
        [VM, VM],
        [pltpu.VMEM((channels, bands, each, pixels), bf16), dmas((channels,))],
        out_specs=HB,
    )(asked, held(tiles_held, pltpu.VMEM))
    recv = lax.all_to_all(send, "band", 0, 0, tiled=True)
    weight_held = call(
        hold_kernel,
        pltpu.VMEM((HELD, pixels, BW), bf16),
        [SM, ANY, HB],
        [dmas((HELD // 8,))],
        cycles=2 * HELD * pixels * BW,
    )(order, held(send, pltpu.HBM), weight_hbm)

    rows = shape((8, C_DEV), bf16)
    chunks = (slots - HELD) // CHUNK
    work = [
        pltpu.VMEM((slots - HELD, pixels, BW), bf16),
        pltpu.VMEM((channels, slots, pixels), f32),
    ]
    to_a, to_b, term = call(
        rim_kernel,
        (rows, rows, shape((channels, slots, BW), f32)),
        [SM, VM, VM, VM, VM, HB],
        work + [dmas((chunks,))],
        vmem=12 << 20,
    )(order, recv, perm, rim, held(weight_held, pltpu.VMEM), weight_hbm)
    wind, others = call(
        rest_kernel,
        (shape((2, R_DEV, C_DEV), bf16), shape((channels - 2, slots, BW), f32)),
        [ANY, SM, VM, VM, VM, VM, HB],
        work + [pltpu.VMEM((2, slots, BW), f32), dmas((chunks,))],
        vmem=12 << 20,
        cycles=slots * pixels * BW,
    )(to_a, order, recv, perm, chosen, term, weight_hbm)

    pairs_a = lambda size: [(i, i ^ 1) for i in range(size)]
    pairs_b = [(i, i + 1 if i % 2 else i - 1) for i in range(1, bands - 1)]
    ring_b = [(i, (i + 1 if i % 2 else i - 1) % lons) for i in range(lons)]
    from_a = lax.ppermute(to_a, "band", pairs_a(bands))
    from_b = lax.ppermute(to_b, "band", pairs_b)
    edge = shape((2 * EXT, 128), bf16)
    ext, to_a, to_b = call(extend_kernel, (shape((2, EXT, C_DEV), f32), edge, edge), [VM, VM, VM])(
        wind, from_a, from_b
    )
    remapped = call(
        finish_kernel, shape((channels, R_DEV, C_DEV), bf16), [ANY, VM, VM, VM], cycles=slots * slots * 16
    )(to_a, chosen, others, wind)
    from_a = lax.ppermute(to_a, "lon", pairs_a(lons))
    from_b = lax.ppermute(to_b, "lon", ring_b)
    smoothed = call(
        functools.partial(smooth_kernel, R_DEV * bands),
        shape((R_DEV, C_DEV), f32),
        [VM, VM, VM, VM],
    )(cosine, ext, from_a, from_b)
    return remapped, smoothed


def solution(mesh):
    in_specs = (
        P(None, ("band", "lon"), None),
        P(("band", "lon")),
        P(("band", "lon")),
        P(("band", "lon"), None, None),
        P(("band", "lon")),
    )
    out_specs = (P(None, "band", "lon"), P("band", "lon"))
    return jax.shard_map(on_device, mesh=mesh, in_specs=in_specs, out_specs=out_specs, check_vma=False)
```

```python
import functools
import math

import jax
import jax.numpy as jnp
from jax import lax
from jax.experimental import pallas as pl
from jax.experimental.pallas import tpu as pltpu
from jax.sharding import PartitionSpec as P

BW = 128
R_DEV = 16
C_DEV = 1024
BLK_ROW = C_DEV // BW
LAT_START = 0.5
HALO = 3
HELD = 88
CHUNK = 24
EXT = 24

VM = pl.BlockSpec(memory_space=pltpu.VMEM)
SM = pl.BlockSpec(memory_space=pltpu.SMEM)
HB = pl.BlockSpec(memory_space=pltpu.HBM)
ANY = pl.BlockSpec(memory_space=pl.ANY)


def dot(a, b):
    return jnp.dot(a, b, preferred_element_type=jnp.float32)


def dot_nt(a, b):
    return lax.dot_general(a, b, (((1,), (1,)), ((), ())), preferred_element_type=jnp.float32)


def iota(shape, dim):
    return lax.broadcasted_iota(jnp.int32, shape, dim)


def as_bf16(flags):
    return flags.astype(jnp.float32).astype(jnp.bfloat16)


def is_odd(axis):
    return lax.axis_index(axis) % 2 == 1


def first_row():
    return lax.axis_index("band") * R_DEV


def route_kernel(per_band, tiles_held, tile_ref, req_ref, pos_ref):
    tile = tile_ref[...]
    slots = tile.shape[1]
    chips = req_ref.shape[0]
    band = tile // per_band
    local = band % 2 * tiles_held + tile % tiles_held
    owner = band // 2
    hit = owner == iota((chips, slots), 0)
    before = as_bf16(iota((slots, slots), 0) < iota((slots, slots), 1))
    earlier = dot(as_bf16(hit), before)
    rank = jnp.sum(jnp.where(hit, earlier, 0.0), axis=0, keepdims=True).astype(jnp.int32)
    place = as_bf16(rank == iota((128, slots), 0))
    high = jnp.where(hit, (local // 16).astype(jnp.float32), 0.0).astype(jnp.bfloat16)
    low = jnp.where(hit, (local % 16).astype(jnp.float32), 0.0).astype(jnp.bfloat16)
    req_ref[...] = (dot_nt(high, place) * 16.0 + dot_nt(low, place)).astype(jnp.int32)
    pos_ref[...] = jnp.broadcast_to(owner * (slots // chips) + rank, (8, slots))


def pick_kernel(req_ref, own_ref, mate_ref, send_hbm, picked, sems):
    channels, tiles, _ = own_ref.shape
    _, chips, each, _ = picked.shape
    asked = jnp.transpose(req_ref[...].astype(jnp.float32)).astype(jnp.int32)
    mine = jnp.where(is_odd("band"), tiles, 0)
    cell = iota((each, tiles), 1)
    columns = [jnp.broadcast_to(asked[:each, d : d + 1], (each, tiles)) for d in range(chips)]
    own = jnp.concatenate([as_bf16(column == cell + mine) for column in columns], axis=0)
    mate = jnp.concatenate([as_bf16(column == cell + (tiles - mine)) for column in columns], axis=0)
    copies = []
    for c in range(0, channels, 2):
        pair = lambda ref: jnp.concatenate([ref[c], ref[c + 1]], axis=1)
        got = (dot(own, pair(own_ref)) + dot(mate, pair(mate_ref))).astype(jnp.bfloat16)
        for k in range(2):
            picked[c + k] = got[:, k * 128 : (k + 1) * 128].reshape(chips, each, 128)
            target = send_hbm.at[:, pl.ds((c + k) * each, each)]
            copies.append(pltpu.make_async_copy(picked.at[c + k], target, sems.at[c + k]))
            copies[-1].start()
    for copy in copies:
        copy.wait()


def stage_kernel(after_ref, source_hbm, held_ref, sems):
    copies = [pltpu.make_async_copy(source_hbm.at[c], held_ref.at[c], sems.at[c]) for c in range(sems.shape[0])]
    for copy in copies:
        copy.start()
    for copy in copies:
        copy.wait()


def fetch_weights(order_ref, weight_hbm, target, sem, first, count, offset):
    for i in range(count):
        slot = order_ref[0, first + i]
        pltpu.make_async_copy(weight_hbm.at[slot], target.at[offset + i], sem).start()


def await_weights(weight_hbm, target, sem, count, offset):
    pltpu.make_async_copy(weight_hbm.at[pl.ds(0, count)], target.at[pl.ds(offset, count)], sem).wait()


def hold_kernel(order_ref, after_ref, weight_hbm, held_ref, sems):
    for g in range(sems.shape[0]):
        fetch_weights(order_ref, weight_hbm, held_ref, sems.at[g], g * 8, 8, g * 8)
    for g in range(sems.shape[0]):
        await_weights(weight_hbm, held_ref, sems.at[g], 8, g * 8)


def select_kernel(
    row_stride, grid_step, after_ref, live_ref, pos_ref, block_ref,
    perm_ref, chosen_ref, rim_ref, order_smem, cosine_ref, order_ref, sem,
):
    slots = pos_ref.shape[1]
    block = block_ref[...]
    row, column = (block // row_stride) % R_DEV, block % BLK_ROW
    lane = iota((1, slots), 1)
    live = lane < live_ref[0]
    at_rim = (column == 0) | (column == BLK_ROW - 1)
    kind = jnp.where(live, jnp.where(at_rim, 0, 1), 2)
    kinds = iota((8, slots), 0)
    hit = kind == kinds
    earlier = dot(as_bf16(hit), as_bf16(iota((slots, slots), 0) < iota((slots, slots), 1)))
    n_rim = jnp.sum(jnp.where(kind == 0, 1.0, 0.0), axis=1, keepdims=True)
    n_live = jnp.sum(jnp.where(kind < 2, 1.0, 0.0), axis=1, keepdims=True)
    start = jnp.where(kinds == 1, n_rim, jnp.where(kinds == 2, n_live, 0.0))
    place = jnp.sum(jnp.where(hit, earlier + start, 0.0), axis=0, keepdims=True).astype(jnp.int32)
    move = as_bf16(place == iota((slots, slots), 0))
    where_from = dot_nt(move, pos_ref[...].astype(jnp.float32).astype(jnp.bfloat16))[:, :1].astype(jnp.int32)
    perm_ref[...] = as_bf16(where_from == iota((slots, slots), 1))
    target = column * R_DEV + row
    rim_target = jnp.where(at_rim, jnp.where(column == 0, row, R_DEV + row), 255)
    facts = [lane, target, live.astype(jnp.int32), rim_target]
    facts = jnp.concatenate([f.astype(jnp.float32) for f in facts + [lane] * 4], axis=0).astype(jnp.bfloat16)
    moved = dot_nt(facts, move).astype(jnp.int32)
    used = moved[2:3] > 0
    chosen_ref[...] = as_bf16((moved[1:2] == iota((BLK_ROW * R_DEV, slots), 0)) & used)
    rim_ref[...] = as_bf16((moved[3:4] == iota(rim_ref.shape, 0)) & used)
    counts = [jnp.broadcast_to(n.astype(jnp.int32), (1, slots)) for n in (n_rim, n_live)]
    order_ref[...] = jnp.concatenate([moved[:1]] + counts + [moved[:1]] * 5, axis=0)
    copy = pltpu.make_async_copy(order_ref, order_smem, sem)
    copy.start()
    row = first_row() - HALO + iota(cosine_ref.shape, 0)
    cosine_ref[...] = jnp.cos(LAT_START + (row.astype(jnp.float32) + 0.5) * grid_step)
    copy.wait()


def add_terms(chosen, rest):
    total = None
    for _ in range(3):
        part = rest.astype(jnp.bfloat16)
        rest = rest - part.astype(jnp.float32)
        share = dot(chosen, part)
        total = share if total is None else total + share
    return total


def add_blocks(chosen, rest):
    total = add_terms(chosen, rest)
    field = jnp.concatenate([total[j * R_DEV : (j + 1) * R_DEV] for j in range(BLK_ROW)], axis=1)
    return field.astype(jnp.bfloat16)


def order_tiles(xs, perm_ref, recv_ref, first, count):
    slots = perm_ref.shape[0]
    each = slots // recv_ref.shape[0]
    for c in range(xs.shape[0]):
        xs[c, first : first + count] = dot(
            perm_ref[first : first + count], recv_ref[:, c * each : (c + 1) * each, :].reshape(slots, 128)
        )


def multiply(xs, eight, terms, first, count):
    channels = xs.shape[0]
    row = iota((8 * channels, 128), 0) % 8
    masks = [as_bf16(row == j) for j in range(8)]
    for g in range(0, count, 8):
        rows = pl.ds(first + g, 8)
        x = jnp.concatenate([xs[c, rows, :] for c in range(channels)], axis=0).astype(jnp.bfloat16)
        spread = jnp.concatenate([x * mask for mask in masks], axis=1)
        got = dot(spread, eight(g))
        for c in range(channels):
            terms[c][rows, :] = got[c * 8 : (c + 1) * 8]


def chunks_of(slots, count):
    return jnp.clip((count - HELD + CHUNK - 1) // CHUNK, 0, (slots - HELD) // CHUNK)


def chunk_steps(order, weight_hbm, weight, xs, terms, sems):
    def fetch(k, carry):
        fetch_weights(order, weight_hbm, weight, sems.at[k], HELD + k * CHUNK, CHUNK, k * CHUNK)
        return carry

    def step(k, carry):
        await_weights(weight_hbm, weight, sems.at[k], CHUNK, k * CHUNK)
        eight = lambda g: weight[pl.ds(k * CHUNK + g, 8)].reshape(8 * 128, 128)
        multiply(xs, eight, terms, pl.multiple_of(HELD + k * CHUNK, 8), CHUNK)
        return carry

    return fetch, step


def rim_kernel(
    order, recv_ref, perm_ref, rim_ref, held_ref, weight_hbm, a_ref, b_ref, term_ref,
    weight, xs, sems,
):
    channels, slots, _ = term_ref.shape
    terms = [term_ref.at[c] for c in range(channels)]
    half = slots // 2
    chunks = chunks_of(slots, order[1, 0])

    fetch, step = chunk_steps(order, weight_hbm, weight, xs, terms, sems)
    lax.fori_loop(0, chunks, fetch, 0)
    order_tiles(xs, perm_ref, recv_ref, 0, half)

    @pl.when(HELD + chunks * CHUNK > half)
    def _():
        order_tiles(xs, perm_ref, recv_ref, half, half)

    for term in terms:
        term[HELD:slots, :] = jnp.zeros((slots - HELD, 128), jnp.float32)
    multiply(xs, lambda g: held_ref[g : g + 8].reshape(8 * 128, 128), terms, 0, HELD)
    lax.fori_loop(0, chunks, step, 0)
    winds = [add_terms(rim_ref[...], term_ref[c]) for c in (2, 3)]
    left = jnp.concatenate([w[:R_DEV] for w in winds], axis=0)
    right = jnp.concatenate([w[R_DEV:] for w in winds], axis=0)
    odd = is_odd("lon")
    a_ref[...] = jnp.where(odd, left, right).astype(jnp.bfloat16)
    b_ref[...] = jnp.where(odd, right, left).astype(jnp.bfloat16)


def rest_kernel(
    after_ref, order, recv_ref, perm_ref, chosen_ref, term_ref, weight_hbm,
    wind_ref, others_ref, weight, xs, term, sems,
):
    channels, slots, _ = term_ref.shape
    terms = [term.at[c - 2] if c in (2, 3) else others_ref.at[c if c < 2 else c - 2] for c in range(channels)]
    first, last = chunks_of(slots, order[1, 0]), chunks_of(slots, order[2, 0])
    fetch, step = chunk_steps(order, weight_hbm, weight, xs, terms, sems)
    lax.fori_loop(first, last, fetch, 0)
    order_tiles(xs, perm_ref, recv_ref, 0, slots)
    for c in range(channels):
        terms[c][...] = term_ref[c]
    lax.fori_loop(first, last, step, 0)
    for w in range(2):
        wind_ref[w] = add_blocks(chosen_ref[...], term[w])


def finish_kernel(after_ref, chosen_ref, others_ref, wind_ref, out_ref):
    for c in range(out_ref.shape[0]):
        if c in (2, 3):
            out_ref[c] = wind_ref[c - 2]
        else:
            out_ref[c] = add_blocks(chosen_ref[...], others_ref[c if c < 2 else c - 2])


def extend_kernel(wind_ref, from_a_ref, from_b_ref, ext_ref, a_ref, b_ref):
    from_a = from_a_ref[...].astype(jnp.float32)
    from_b = from_b_ref[...].astype(jnp.float32)
    odd = is_odd("lon")
    left = jnp.where(odd, from_a, from_b)
    right = jnp.where(odd, from_b, from_a)
    winds = []
    for w in range(2):
        rows = slice(w * R_DEV, (w + 1) * R_DEV)
        winds.append(jnp.concatenate([left[rows], wind_ref[w].astype(jnp.float32), right[rows]], axis=1))
        ext_ref[w] = winds[w]
    pad = jnp.zeros((8 - 2 * HALO, winds[0].shape[1]), jnp.float32)
    first = jnp.concatenate([w[:HALO] for w in winds] + [pad], axis=0)
    last = jnp.concatenate([w[R_DEV - HALO :] for w in winds] + [pad], axis=0)
    odd = is_odd("band")
    a_ref[...] = jnp.where(odd, first, last).astype(jnp.bfloat16)
    b_ref[...] = jnp.where(odd, last, first).astype(jnp.bfloat16)


def smooth(x):
    rows, columns = x.shape
    x = 2.0 * x + (pltpu.roll(x, 1, 0) + pltpu.roll(x, rows - 1, 0))
    x = 2.0 * x + (pltpu.roll(x, 1, 1) + pltpu.roll(x, columns - 1, 1))
    return x * (1.0 / 16.0)


def smooth_kernel(all_rows, cosine_ref, ext_ref, from_a_ref, from_b_ref, out_ref):
    from_a = from_a_ref[...].astype(jnp.float32)
    from_b = from_b_ref[...].astype(jnp.float32)
    odd = is_odd("band")
    above = jnp.where(odd, from_a, from_b)
    below = jnp.where(odd, from_b, from_a)
    pad = jnp.zeros((EXT - R_DEV - 2 * HALO, above.shape[1]), jnp.float32)
    east, north = (
        jnp.concatenate([above[w * HALO : (w + 1) * HALO], ext_ref[w], below[w * HALO : (w + 1) * HALO], pad], axis=0)
        for w in range(2)
    )
    rows, columns = east.shape
    row = first_row() - HALO + iota((rows, 128), 0)
    inside = jnp.tile((row >= 0) & (row < all_rows), (1, columns // 128))
    cosine = cosine_ref[...]
    scaled = east * jnp.tile(cosine, (1, columns // 128))
    half = jnp.tile(0.5 / cosine, (1, columns // 128))
    along = pltpu.roll(north, columns - 1, 1) - pltpu.roll(north, 1, 1)
    across = pltpu.roll(scaled, rows - 1, 0) - pltpu.roll(scaled, 1, 0)
    field = jnp.where(inside, (along - across) * half, 0.0)
    field = jnp.where(inside, smooth(field), 0.0)
    field = smooth(field)
    out_ref[...] = field[HALO : HALO + R_DEV, 128 : 128 + C_DEV]


def call(kernel, outs, ins, scratch=(), vmem=2 << 20, cycles=0, out_specs=None):
    return pl.pallas_call(
        kernel,
        out_shape=outs,
        in_specs=ins,
        out_specs=out_specs or jax.tree.map(lambda _: VM, outs),
        scratch_shapes=scratch,
        compiler_params=pltpu.CompilerParams(vmem_limit_bytes=vmem),
        cost_estimate=pl.CostEstimate(flops=cycles, bytes_accessed=cycles, transcendentals=0) if cycles else None,
    )


def on_device(src_tiles, ent_tile, ent_block, ent_weight, live_count):
    bands, lons = lax.axis_size("band"), lax.axis_size("lon")
    channels, tiles, pixels = src_tiles.shape
    slots = ent_tile.shape[0]
    each = 2 * slots // bands
    shape = jax.ShapeDtypeStruct
    bf16, f32, i32 = jnp.bfloat16, jnp.float32, jnp.int32
    dmas = pltpu.SemaphoreType.DMA
    held = pltpu.with_memory_space_constraint

    chips = bands // 2
    same_core = [[chip * 2 + core for chip in range(chips)] for core in range(2)]
    exchange = lambda x: lax.all_to_all(x, "band", 0, 0, tiled=True, axis_index_groups=same_core)
    pairs_a = lambda size: [(i, i ^ 1) for i in range(size)]
    mate_tiles = lax.ppermute(src_tiles, "band", pairs_a(bands))
    req, pos = call(
        functools.partial(route_kernel, lons * tiles, tiles),
        (shape((chips, 128), i32), shape((8, slots), i32)),
        [VM],
    )(ent_tile.reshape(1, slots))
    asked = exchange(req)
    own_tiles = call(
        stage_kernel, pltpu.VMEM(src_tiles.shape, bf16), [ANY, HB], [dmas((channels,))], cycles=2 * src_tiles.size
    )(req, held(src_tiles, pltpu.HBM))
    send = call(
        pick_kernel,
        pltpu.HBM((chips, channels * each, pixels), bf16),
        [VM, VM, VM],
        [pltpu.VMEM((channels, chips, each, pixels), bf16), dmas((channels,))],
        out_specs=HB,
    )(asked, held(own_tiles, pltpu.VMEM), held(mate_tiles, pltpu.VMEM))
    perm, chosen, rim, order, cosine = call(
        functools.partial(select_kernel, BLK_ROW * lons, 2.0 * math.pi / (C_DEV * lons)),
        (
            shape((slots, slots), bf16),
            shape((BLK_ROW * R_DEV, slots), bf16),
            shape((2 * R_DEV, slots), bf16),
            pltpu.SMEM((8, slots), i32),
            shape((EXT, 128), f32),
        ),
        [ANY, SM, VM, VM],
        [pltpu.VMEM((8, slots), i32), dmas],
        out_specs=(VM, VM, VM, SM, VM),
        cycles=slots * slots * 8,
    )(held(send, pltpu.HBM), live_count, pos, ent_block.reshape(1, slots))
    order = held(order, pltpu.SMEM)
    weight_hbm = held(ent_weight, pltpu.HBM)
    recv = exchange(send)
    weight_held = call(
        hold_kernel,
        pltpu.VMEM((HELD, pixels, BW), bf16),
        [SM, ANY, HB],
        [dmas((HELD // 8,))],
        cycles=2 * HELD * pixels * BW,
    )(order, held(send, pltpu.HBM), weight_hbm)

    sides, rows = shape((2 * R_DEV, 128), bf16), shape((8, C_DEV + 256), bf16)
    chunks = (slots - HELD) // CHUNK
    work = [
        pltpu.VMEM((slots - HELD, pixels, BW), bf16),
        pltpu.VMEM((channels, slots, pixels), f32),
    ]
    to_a, to_b, term = call(
        rim_kernel,
        (sides, sides, shape((channels, slots, BW), f32)),
        [SM, VM, VM, VM, VM, HB],
        work + [dmas((chunks,))],
        vmem=12 << 20,
    )(order, recv, perm, rim, held(weight_held, pltpu.VMEM), weight_hbm)
    wind, others = call(
        rest_kernel,
        (shape((2, R_DEV, C_DEV), bf16), shape((channels - 2, slots, BW), f32)),
        [ANY, SM, VM, VM, VM, VM, HB],
        work + [pltpu.VMEM((2, slots, BW), f32), dmas((chunks,))],
        vmem=12 << 20,
        cycles=slots * pixels * BW,
    )(to_a, order, recv, perm, chosen, term, weight_hbm)

    pairs_b = [(i, i + 1 if i % 2 else i - 1) for i in range(1, bands - 1)]
    ring_b = [(i, (i + 1 if i % 2 else i - 1) % lons) for i in range(lons)]
    from_a = lax.ppermute(to_a, "lon", pairs_a(lons))
    from_b = lax.ppermute(to_b, "lon", ring_b)
    ext, to_a, to_b = call(extend_kernel, (shape((2, R_DEV, C_DEV + 256), f32), rows, rows), [VM, VM, VM])(
        wind, from_a, from_b
    )
    remapped = call(
        finish_kernel, shape((channels, R_DEV, C_DEV), bf16), [ANY, VM, VM, VM], cycles=slots * slots * 16
    )(to_a, chosen, others, wind)
    from_a = lax.ppermute(to_a, "band", pairs_a(bands))
    from_b = lax.ppermute(to_b, "band", pairs_b)
    smoothed = call(
        functools.partial(smooth_kernel, R_DEV * bands),
        shape((R_DEV, C_DEV), f32),
        [VM, VM, VM, VM],
    )(cosine, ext, from_a, from_b)
    return remapped, smoothed


def solution(mesh):
    in_specs = (
        P(None, ("band", "lon"), None),
        P(("band", "lon")),
        P(("band", "lon")),
        P(("band", "lon"), None, None),
        P(("band", "lon")),
    )
    out_specs = (P(None, "band", "lon"), P("band", "lon"))
    return jax.shard_map(on_device, mesh=mesh, in_specs=in_specs, out_specs=out_specs, check_vma=False)
```

```python
import functools
import math

import jax
import jax.numpy as jnp
from jax import lax
from jax.experimental import pallas as pl
from jax.experimental.pallas import tpu as pltpu
from jax.sharding import PartitionSpec as P

BW = 128
R_DEV = 16
C_DEV = 1024
BLK_ROW = C_DEV // BW
LAT_START = 0.5
HALO = 3
HELD = 88
CHUNK = 24
EXT = 24

VM = pl.BlockSpec(memory_space=pltpu.VMEM)
SM = pl.BlockSpec(memory_space=pltpu.SMEM)
HB = pl.BlockSpec(memory_space=pltpu.HBM)
ANY = pl.BlockSpec(memory_space=pl.ANY)


def dot(a, b):
    return jnp.dot(a, b, preferred_element_type=jnp.float32)


def dot_nt(a, b):
    return lax.dot_general(a, b, (((1,), (1,)), ((), ())), preferred_element_type=jnp.float32)


def iota(shape, dim):
    return lax.broadcasted_iota(jnp.int32, shape, dim)


def as_bf16(flags):
    return flags.astype(jnp.float32).astype(jnp.bfloat16)


def is_odd(axis):
    return lax.axis_index(axis) % 2 == 1


def first_row():
    return lax.axis_index("band") * R_DEV


def route_kernel(per_band, tiles_held, tile_hbm, src_hbm, req_ref, pos_ref, src_ref, tile_ref, tile_sem, sems):
    tile_copy = pltpu.make_async_copy(tile_hbm, tile_ref, tile_sem)
    tile_copy.start()
    copies = []
    for h in range(2):
        half = pl.ds(h * (src_ref.shape[0] // 2), src_ref.shape[0] // 2)
        copies.append(pltpu.make_async_copy(src_hbm.at[half], src_ref.at[half], sems.at[h]))
        copies[-1].start()
    tile_copy.wait()
    tile = tile_ref[...]
    slots = tile.shape[1]
    chips = req_ref.shape[0]
    band = tile // per_band
    local = band % 2 * tiles_held + tile % tiles_held
    owner = band // 2
    hit = owner == iota((chips, slots), 0)
    before = as_bf16(iota((slots, slots), 0) < iota((slots, slots), 1))
    earlier = dot(as_bf16(hit), before)
    rank = jnp.sum(jnp.where(hit, earlier, 0.0), axis=0, keepdims=True).astype(jnp.int32)
    place = as_bf16(rank == iota((128, slots), 0))
    high = jnp.where(hit, (local // 16).astype(jnp.float32), 0.0).astype(jnp.bfloat16)
    low = jnp.where(hit, (local % 16).astype(jnp.float32), 0.0).astype(jnp.bfloat16)
    req_ref[...] = (dot_nt(high, place) * 16.0 + dot_nt(low, place)).astype(jnp.int32)
    pos_ref[...] = jnp.broadcast_to(owner * (slots // chips) + rank, (8, slots))
    for copy in copies:
        copy.wait()


def pick_kernel(req_ref, own_ref, mate_ref, send_hbm, picked, sems):
    channels, tiles, _ = own_ref.shape
    _, chips, each, _ = picked.shape
    asked = jnp.transpose(req_ref[...].astype(jnp.float32)).astype(jnp.int32)
    mine = jnp.where(is_odd("band"), tiles, 0)
    cell = iota((each, tiles), 1)
    columns = [jnp.broadcast_to(asked[:each, d : d + 1], (each, tiles)) for d in range(chips)]
    own = jnp.concatenate([as_bf16(column == cell + mine) for column in columns], axis=0)
    mate = jnp.concatenate([as_bf16(column == cell + (tiles - mine)) for column in columns], axis=0)
    copies = []
    for c in range(0, channels, 2):
        pair = lambda ref: jnp.concatenate([ref[c], ref[c + 1]], axis=1)
        got = (dot(own, pair(own_ref)) + dot(mate, pair(mate_ref))).astype(jnp.bfloat16)
        for k in range(2):
            picked[c + k] = got[:, k * 128 : (k + 1) * 128].reshape(chips, each, 128)
            target = send_hbm.at[:, pl.ds((c + k) * each, each)]
            copies.append(pltpu.make_async_copy(picked.at[c + k], target, sems.at[c + k]))
            copies[-1].start()
    for copy in copies:
        copy.wait()


def fetch_weights(order_ref, weight_hbm, target, sem, first, count, offset):
    for i in range(count):
        slot = order_ref[0, first + i]
        pltpu.make_async_copy(weight_hbm.at[slot], target.at[offset + i], sem).start()


def await_weights(weight_hbm, target, sem, count, offset):
    pltpu.make_async_copy(weight_hbm.at[pl.ds(0, count)], target.at[pl.ds(offset, count)], sem).wait()


def hold_kernel(order_ref, after_ref, weight_hbm, held_ref, sems):
    for g in range(sems.shape[0]):
        fetch_weights(order_ref, weight_hbm, held_ref, sems.at[g], g * 8, 8, g * 8)
    for g in range(sems.shape[0]):
        await_weights(weight_hbm, held_ref, sems.at[g], 8, g * 8)


def select_kernel(
    row_stride, grid_step, after_ref, live_ref, pos_ref, block_ref,
    perm_ref, chosen_ref, rim_ref, order_smem, cosine_ref, order_ref, sem,
):
    slots = pos_ref.shape[1]
    block = block_ref[...]
    row, column = (block // row_stride) % R_DEV, block % BLK_ROW
    lane = iota((1, slots), 1)
    live = lane < live_ref[0]
    at_rim = (column == 0) | (column == BLK_ROW - 1)
    kind = jnp.where(live, jnp.where(at_rim, 0, 1), 2)
    kinds = iota((8, slots), 0)
    hit = kind == kinds
    earlier = dot(as_bf16(hit), as_bf16(iota((slots, slots), 0) < iota((slots, slots), 1)))
    n_rim = jnp.sum(jnp.where(kind == 0, 1.0, 0.0), axis=1, keepdims=True)
    n_live = jnp.sum(jnp.where(kind < 2, 1.0, 0.0), axis=1, keepdims=True)
    start = jnp.where(kinds == 1, n_rim, jnp.where(kinds == 2, n_live, 0.0))
    place = jnp.sum(jnp.where(hit, earlier + start, 0.0), axis=0, keepdims=True).astype(jnp.int32)
    move = as_bf16(place == iota((slots, slots), 0))
    where_from = dot_nt(move, pos_ref[...].astype(jnp.float32).astype(jnp.bfloat16))[:, :1].astype(jnp.int32)
    perm_ref[...] = as_bf16(where_from == iota((slots, slots), 1))
    target = column * R_DEV + row
    rim_target = jnp.where(at_rim, jnp.where(column == 0, row, R_DEV + row), 255)
    facts = [lane, target, live.astype(jnp.int32), rim_target]
    facts = jnp.concatenate([f.astype(jnp.float32) for f in facts + [lane] * 4], axis=0).astype(jnp.bfloat16)
    moved = dot_nt(facts, move).astype(jnp.int32)
    used = moved[2:3] > 0
    chosen_ref[...] = as_bf16((moved[1:2] == iota((BLK_ROW * R_DEV, slots), 0)) & used)
    rim_ref[...] = as_bf16((moved[3:4] == iota(rim_ref.shape, 0)) & used)
    counts = [jnp.broadcast_to(n.astype(jnp.int32), (1, slots)) for n in (n_rim, n_live)]
    order_ref[...] = jnp.concatenate([moved[:1]] + counts + [moved[:1]] * 5, axis=0)
    copy = pltpu.make_async_copy(order_ref, order_smem, sem)
    copy.start()
    row = first_row() - HALO + iota(cosine_ref.shape, 0)
    cosine_ref[...] = jnp.cos(LAT_START + (row.astype(jnp.float32) + 0.5) * grid_step)
    copy.wait()


def add_terms(chosen, rest):
    total = None
    for _ in range(3):
        part = rest.astype(jnp.bfloat16)
        rest = rest - part.astype(jnp.float32)
        share = dot(chosen, part)
        total = share if total is None else total + share
    return total


def add_blocks(chosen, rest):
    total = add_terms(chosen, rest)
    field = jnp.concatenate([total[j * R_DEV : (j + 1) * R_DEV] for j in range(BLK_ROW)], axis=1)
    return field.astype(jnp.bfloat16)


def order_tiles(xs, perm_ref, recv_ref, channels, first, count):
    slots = perm_ref.shape[0]
    each = slots // recv_ref.shape[0]
    for i, c in enumerate(channels):
        xs[i, first : first + count] = dot(
            perm_ref[first : first + count], recv_ref[:, c * each : (c + 1) * each, :].reshape(slots, 128)
        )


def multiply(xs, eight, terms, first, count, channels=None):
    channels = channels or range(xs.shape[0])
    row = iota((8 * len(channels), 128), 0) % 8
    masks = [as_bf16(row == j) for j in range(8)]
    for g in range(0, count, 8):
        rows = pl.ds(first + g, 8)
        x = jnp.concatenate([xs[c, rows, :] for c in channels], axis=0).astype(jnp.bfloat16)
        spread = jnp.concatenate([x * mask for mask in masks], axis=1)
        got = dot(spread, eight(g))
        for i, c in enumerate(channels):
            terms[c][rows, :] = got[i * 8 : (i + 1) * 8]


def chunks_of(slots, count):
    return jnp.clip((count - HELD + CHUNK - 1) // CHUNK, 0, (slots - HELD) // CHUNK)


def chunk_steps(order, weight_hbm, weight, xs, terms, sems):
    def fetch(k, carry):
        fetch_weights(order, weight_hbm, weight, sems.at[k], HELD + k * CHUNK, CHUNK, k * CHUNK)
        return carry

    def step(k, carry):
        await_weights(weight_hbm, weight, sems.at[k], CHUNK, k * CHUNK)
        eight = lambda g: weight[pl.ds(k * CHUNK + g, 8)].reshape(8 * 128, 128)
        multiply(xs, eight, terms, pl.multiple_of(HELD + k * CHUNK, 8), CHUNK)
        return carry

    return fetch, step


def rim_kernel(
    order, recv_ref, perm_ref, rim_ref, held_ref, weight_hbm, a_ref, b_ref, term_ref,
    weight, xs, sems,
):
    slots = term_ref.shape[1]
    terms = [term_ref.at[w] for w in range(2)]
    half = slots // 2
    chunks = chunks_of(slots, order[1, 0])
    fetch, step = chunk_steps(order, weight_hbm, weight, xs, terms, sems)
    lax.fori_loop(0, chunks, fetch, 0)
    order_tiles(xs, perm_ref, recv_ref, (2, 3), 0, half)

    @pl.when(HELD + chunks * CHUNK > half)
    def _():
        order_tiles(xs, perm_ref, recv_ref, (2, 3), half, half)

    for term in terms:
        term[HELD:slots, :] = jnp.zeros((slots - HELD, 128), jnp.float32)
    multiply(xs, lambda g: held_ref[g : g + 8].reshape(8 * 128, 128), terms, 0, HELD)
    lax.fori_loop(0, chunks, step, 0)
    winds = [add_terms(rim_ref[...], term[...]) for term in terms]
    left = jnp.concatenate([w[:R_DEV] for w in winds], axis=0)
    right = jnp.concatenate([w[R_DEV:] for w in winds], axis=0)
    odd = is_odd("lon")
    a_ref[...] = jnp.where(odd, left, right).astype(jnp.bfloat16)
    b_ref[...] = jnp.where(odd, right, left).astype(jnp.bfloat16)


def rest_kernel(
    after_ref, order, recv_ref, perm_ref, chosen_ref, term_ref, held_ref, weight_hbm,
    wind_ref, others_ref, weight, xs, term, sems,
):
    slots = term_ref.shape[1]
    channels = 2 + others_ref.shape[0]
    terms = [term.at[c - 2] if c in (2, 3) else others_ref.at[c if c < 2 else c - 2] for c in range(channels)]
    last = chunks_of(slots, order[2, 0])
    fetch, step = chunk_steps(order, weight_hbm, weight, xs, terms, sems)

    lax.fori_loop(0, last, fetch, 0)
    order_tiles(xs, perm_ref, recv_ref, range(channels), 0, slots)
    for target in terms:
        target[HELD:slots, :] = jnp.zeros((slots - HELD, 128), jnp.float32)
    for w in range(2):
        term[w, :HELD] = term_ref[w, :HELD]
    eight = lambda g: held_ref[g : g + 8].reshape(8 * 128, 128)
    multiply(xs, eight, terms, 0, HELD, [c for c in range(channels) if c not in (2, 3)])
    lax.fori_loop(0, last, step, 0)
    for w in range(2):
        wind_ref[w] = add_blocks(chosen_ref[...], term[w])


def finish_kernel(after_ref, chosen_ref, others_ref, wind_ref, out_ref):
    for c in range(out_ref.shape[0]):
        if c in (2, 3):
            out_ref[c] = wind_ref[c - 2]
        else:
            out_ref[c] = add_blocks(chosen_ref[...], others_ref[c if c < 2 else c - 2])


def extend_kernel(wind_ref, from_a_ref, from_b_ref, ext_ref, a_ref, b_ref):
    from_a = from_a_ref[...].astype(jnp.float32)
    from_b = from_b_ref[...].astype(jnp.float32)
    odd = is_odd("lon")
    left = jnp.where(odd, from_a, from_b)
    right = jnp.where(odd, from_b, from_a)
    winds = []
    for w in range(2):
        rows = slice(w * R_DEV, (w + 1) * R_DEV)
        winds.append(jnp.concatenate([left[rows], wind_ref[w].astype(jnp.float32), right[rows]], axis=1))
        ext_ref[w] = winds[w]
    pad = jnp.zeros((8 - 2 * HALO, winds[0].shape[1]), jnp.float32)
    first = jnp.concatenate([w[:HALO] for w in winds] + [pad], axis=0)
    last = jnp.concatenate([w[R_DEV - HALO :] for w in winds] + [pad], axis=0)
    odd = is_odd("band")
    a_ref[...] = jnp.where(odd, first, last).astype(jnp.bfloat16)
    b_ref[...] = jnp.where(odd, last, first).astype(jnp.bfloat16)


def smooth(x):
    rows, columns = x.shape
    x = 2.0 * x + (pltpu.roll(x, 1, 0) + pltpu.roll(x, rows - 1, 0))
    x = 2.0 * x + (pltpu.roll(x, 1, 1) + pltpu.roll(x, columns - 1, 1))
    return x * (1.0 / 16.0)


def smooth_kernel(all_rows, cosine_ref, ext_ref, from_a_ref, from_b_ref, out_ref):
    from_a = from_a_ref[...].astype(jnp.float32)
    from_b = from_b_ref[...].astype(jnp.float32)
    odd = is_odd("band")
    above = jnp.where(odd, from_a, from_b)
    below = jnp.where(odd, from_b, from_a)
    pad = jnp.zeros((EXT - R_DEV - 2 * HALO, above.shape[1]), jnp.float32)
    east, north = (
        jnp.concatenate([above[w * HALO : (w + 1) * HALO], ext_ref[w], below[w * HALO : (w + 1) * HALO], pad], axis=0)
        for w in range(2)
    )
    rows, columns = east.shape
    row = first_row() - HALO + iota((rows, 128), 0)
    inside = jnp.tile((row >= 0) & (row < all_rows), (1, columns // 128))
    cosine = cosine_ref[...]
    scaled = east * jnp.tile(cosine, (1, columns // 128))
    half = jnp.tile(0.5 / cosine, (1, columns // 128))
    along = pltpu.roll(north, columns - 1, 1) - pltpu.roll(north, 1, 1)
    across = pltpu.roll(scaled, rows - 1, 0) - pltpu.roll(scaled, 1, 0)
    field = jnp.where(inside, (along - across) * half, 0.0)
    field = jnp.where(inside, smooth(field), 0.0)
    field = smooth(field)
    out_ref[...] = field[HALO : HALO + R_DEV, 128 : 128 + C_DEV]


def call(kernel, outs, ins, scratch=(), vmem=2 << 20, cycles=0, out_specs=None):
    return pl.pallas_call(
        kernel,
        out_shape=outs,
        in_specs=ins,
        out_specs=out_specs or jax.tree.map(lambda _: VM, outs),
        scratch_shapes=scratch,
        compiler_params=pltpu.CompilerParams(vmem_limit_bytes=vmem),
        cost_estimate=pl.CostEstimate(flops=cycles, bytes_accessed=cycles, transcendentals=0) if cycles else None,
    )


def on_device(src_tiles, ent_tile, ent_block, ent_weight, live_count):
    bands, lons = lax.axis_size("band"), lax.axis_size("lon")
    channels, tiles, pixels = src_tiles.shape
    slots = ent_tile.shape[0]
    each = 2 * slots // bands
    shape = jax.ShapeDtypeStruct
    bf16, f32, i32 = jnp.bfloat16, jnp.float32, jnp.int32
    dmas = pltpu.SemaphoreType.DMA
    held = pltpu.with_memory_space_constraint

    chips = bands // 2
    same_core = [[chip * 2 + core for chip in range(chips)] for core in range(2)]
    exchange = lambda x: lax.all_to_all(x, "band", 0, 0, tiled=True, axis_index_groups=same_core)
    pairs_a = lambda size: [(i, i ^ 1) for i in range(size)]
    mate_tiles = lax.ppermute(src_tiles, "band", pairs_a(bands))
    req, pos, own_tiles = call(
        functools.partial(route_kernel, lons * tiles, tiles),
        (shape((chips, 128), i32), shape((8, slots), i32), shape(src_tiles.shape, bf16)),
        [HB, HB],
        [pltpu.VMEM((1, slots), i32), dmas, dmas((2,))],
    )(held(ent_tile.reshape(1, slots), pltpu.HBM), held(src_tiles, pltpu.HBM))
    asked = exchange(req)
    send = call(
        pick_kernel,
        pltpu.HBM((chips, channels * each, pixels), bf16),
        [VM, VM, VM],
        [pltpu.VMEM((channels, chips, each, pixels), bf16), dmas((channels,))],
        out_specs=HB,
    )(asked, held(own_tiles, pltpu.VMEM), held(mate_tiles, pltpu.VMEM))
    perm, chosen, rim, order, cosine = call(
        functools.partial(select_kernel, BLK_ROW * lons, 2.0 * math.pi / (C_DEV * lons)),
        (
            shape((slots, slots), bf16),
            shape((BLK_ROW * R_DEV, slots), bf16),
            shape((2 * R_DEV, slots), bf16),
            pltpu.SMEM((8, slots), i32),
            shape((EXT, 128), f32),
        ),
        [ANY, SM, VM, VM],
        [pltpu.VMEM((8, slots), i32), dmas],
        out_specs=(VM, VM, VM, SM, VM),
        cycles=slots * slots * 8,
    )(held(send, pltpu.HBM), live_count, pos, ent_block.reshape(1, slots))
    order = held(order, pltpu.SMEM)
    weight_hbm = held(ent_weight, pltpu.HBM)
    recv = exchange(send)
    weight_held = call(
        hold_kernel,
        pltpu.VMEM((HELD, pixels, BW), bf16),
        [SM, ANY, HB],
        [dmas((HELD // 8,))],
        cycles=2 * HELD * pixels * BW,
    )(order, held(send, pltpu.HBM), weight_hbm)

    sides, rows = shape((2 * R_DEV, 128), bf16), shape((8, C_DEV + 256), bf16)
    chunks = (slots - HELD) // CHUNK
    weight = pltpu.VMEM((slots - HELD, pixels, BW), bf16)
    per_slot = lambda count: pltpu.VMEM((count, slots, 128), f32)
    weight_held = held(weight_held, pltpu.VMEM)
    to_a, to_b, term = call(
        rim_kernel,
        (sides, sides, shape((2, slots, BW), f32)),
        [SM, VM, VM, VM, VM, HB],
        [weight, per_slot(2), dmas((chunks,))],
        vmem=12 << 20,
    )(order, recv, perm, rim, weight_held, weight_hbm)
    wind, others = call(
        rest_kernel,
        (shape((2, R_DEV, C_DEV), bf16), shape((channels - 2, slots, BW), f32)),
        [ANY, SM, VM, VM, VM, VM, VM, HB],
        [weight, per_slot(channels), per_slot(2), dmas((chunks,))],
        vmem=12 << 20,
        cycles=slots * pixels * BW,
    )(to_a, order, recv, perm, chosen, term, weight_held, weight_hbm)

    pairs_b = [(i, i + 1 if i % 2 else i - 1) for i in range(1, bands - 1)]
    ring_b = [(i, (i + 1 if i % 2 else i - 1) % lons) for i in range(lons)]
    from_a = lax.ppermute(to_a, "lon", pairs_a(lons))
    from_b = lax.ppermute(to_b, "lon", ring_b)
    ext, to_a, to_b = call(extend_kernel, (shape((2, R_DEV, C_DEV + 256), f32), rows, rows), [VM, VM, VM])(
        wind, from_a, from_b
    )
    remapped = call(
        finish_kernel, shape((channels, R_DEV, C_DEV), bf16), [ANY, VM, VM, VM], cycles=slots * slots * 16
    )(to_a, chosen, others, wind)
    from_a = lax.ppermute(to_a, "band", pairs_a(bands))
    from_b = lax.ppermute(to_b, "band", pairs_b)
    smoothed = call(
        functools.partial(smooth_kernel, R_DEV * bands),
        shape((R_DEV, C_DEV), f32),
        [VM, VM, VM, VM],
    )(cosine, ext, from_a, from_b)
    return remapped, smoothed


def solution(mesh):
    in_specs = (
        P(None, ("band", "lon"), None),
        P(("band", "lon")),
        P(("band", "lon")),
        P(("band", "lon"), None, None),
        P(("band", "lon")),
    )
    out_specs = (P(None, "band", "lon"), P("band", "lon"))
    return jax.shard_map(on_device, mesh=mesh, in_specs=in_specs, out_specs=out_specs, check_vma=False)
```

```python
import functools
import math

import jax
import jax.numpy as jnp
from jax import lax
from jax.experimental import pallas as pl
from jax.experimental.pallas import tpu as pltpu
from jax.sharding import PartitionSpec as P

BW = 128
R_DEV = 16
C_DEV = 1024
BLK_ROW = C_DEV // BW
LAT_START = 0.5
HALO = 3
HELD = 88
CHUNK = 24
EXT = 24

VM = pl.BlockSpec(memory_space=pltpu.VMEM)
SM = pl.BlockSpec(memory_space=pltpu.SMEM)
HB = pl.BlockSpec(memory_space=pltpu.HBM)
ANY = pl.BlockSpec(memory_space=pl.ANY)


def dot(a, b):
    return jnp.dot(a, b, preferred_element_type=jnp.float32)


def dot_nt(a, b):
    return lax.dot_general(a, b, (((1,), (1,)), ((), ())), preferred_element_type=jnp.float32)


def iota(shape, dim):
    return lax.broadcasted_iota(jnp.int32, shape, dim)


def as_bf16(flags):
    return flags.astype(jnp.float32).astype(jnp.bfloat16)


def is_odd(axis):
    return lax.axis_index(axis) % 2 == 1


def first_row():
    return lax.axis_index("band") * R_DEV


def route_kernel(per_band, tiles_held, tile_hbm, src_hbm, req_ref, pos_ref, src_ref, tile_ref, tile_sem, sems):
    tile_copy = pltpu.make_async_copy(tile_hbm, tile_ref, tile_sem)
    tile_copy.start()
    copies = []
    for h in range(2):
        half = pl.ds(h * (src_ref.shape[0] // 2), src_ref.shape[0] // 2)
        copies.append(pltpu.make_async_copy(src_hbm.at[half], src_ref.at[half], sems.at[h]))
        copies[-1].start()
    tile_copy.wait()
    tile = tile_ref[...]
    slots = tile.shape[1]
    chips = req_ref.shape[0]
    band = tile // per_band
    local = band % 2 * tiles_held + tile % tiles_held
    owner = band // 2
    hit = owner == iota((chips, slots), 0)
    before = as_bf16(iota((slots, slots), 0) < iota((slots, slots), 1))
    earlier = dot(as_bf16(hit), before)
    rank = jnp.sum(jnp.where(hit, earlier, 0.0), axis=0, keepdims=True).astype(jnp.int32)
    place = as_bf16(rank == iota((128, slots), 0))
    high = jnp.where(hit, (local // 16).astype(jnp.float32), 0.0).astype(jnp.bfloat16)
    low = jnp.where(hit, (local % 16).astype(jnp.float32), 0.0).astype(jnp.bfloat16)
    req_ref[...] = (dot_nt(high, place) * 16.0 + dot_nt(low, place)).astype(jnp.int32)
    pos_ref[...] = jnp.broadcast_to(owner * (slots // chips) + rank, (8, slots))
    for copy in copies:
        copy.wait()


def pick_kernel(req_ref, own_ref, mate_ref, send_hbm, picked, sems):
    channels, tiles, _ = own_ref.shape
    _, chips, each, _ = picked.shape
    asked = jnp.transpose(req_ref[...].astype(jnp.float32)).astype(jnp.int32)
    mine = jnp.where(is_odd("band"), tiles, 0)
    cell = iota((each, tiles), 1)
    columns = [jnp.broadcast_to(asked[:each, d : d + 1], (each, tiles)) for d in range(chips)]
    own = jnp.concatenate([as_bf16(column == cell + mine) for column in columns], axis=0)
    mate = jnp.concatenate([as_bf16(column == cell + (tiles - mine)) for column in columns], axis=0)
    copies = []
    for c in range(0, channels, 2):
        pair = lambda ref: jnp.concatenate([ref[c], ref[c + 1]], axis=1)
        got = (dot(own, pair(own_ref)) + dot(mate, pair(mate_ref))).astype(jnp.bfloat16)
        for k in range(2):
            picked[c + k] = got[:, k * 128 : (k + 1) * 128].reshape(chips, each, 128)
            target = send_hbm.at[:, pl.ds((c + k) * each, each)]
            copies.append(pltpu.make_async_copy(picked.at[c + k], target, sems.at[c + k]))
            copies[-1].start()
    for copy in copies:
        copy.wait()


def fetch_weights(order_ref, weight_hbm, target, sem, first, count, offset):
    for i in range(count):
        slot = order_ref[0, first + i]
        pltpu.make_async_copy(weight_hbm.at[slot], target.at[offset + i], sem).start()


def await_weights(weight_hbm, target, sem, count, offset):
    pltpu.make_async_copy(weight_hbm.at[pl.ds(0, count)], target.at[pl.ds(offset, count)], sem).wait()


def hold_kernel(order_ref, after_ref, weight_hbm, held_ref, sems):
    for g in range(sems.shape[0]):
        fetch_weights(order_ref, weight_hbm, held_ref, sems.at[g], g * 8, 8, g * 8)
    for g in range(sems.shape[0]):
        await_weights(weight_hbm, held_ref, sems.at[g], 8, g * 8)


def select_kernel(
    row_stride, grid_step, after_ref, live_ref, pos_ref, block_ref,
    perm_ref, chosen_ref, rim_ref, order_smem, cosine_ref, order_ref, sem,
):
    slots = pos_ref.shape[1]
    block = block_ref[...]
    row, column = (block // row_stride) % R_DEV, block % BLK_ROW
    lane = iota((1, slots), 1)
    live = lane < live_ref[0]
    at_rim = (column == 0) | (column == BLK_ROW - 1)
    kind = jnp.where(live, jnp.where(at_rim, 0, 1), 2)
    kinds = iota((8, slots), 0)
    hit = kind == kinds
    earlier = dot(as_bf16(hit), as_bf16(iota((slots, slots), 0) < iota((slots, slots), 1)))
    n_rim = jnp.sum(jnp.where(kind == 0, 1.0, 0.0), axis=1, keepdims=True)
    n_live = jnp.sum(jnp.where(kind < 2, 1.0, 0.0), axis=1, keepdims=True)
    start = jnp.where(kinds == 1, n_rim, jnp.where(kinds == 2, n_live, 0.0))
    place = jnp.sum(jnp.where(hit, earlier + start, 0.0), axis=0, keepdims=True).astype(jnp.int32)
    move = as_bf16(place == iota((slots, slots), 0))
    where_from = dot_nt(move, pos_ref[...].astype(jnp.float32).astype(jnp.bfloat16))[:, :1].astype(jnp.int32)
    perm_ref[...] = as_bf16(where_from == iota((slots, slots), 1))
    target = column * R_DEV + row
    rim_target = jnp.where(at_rim, jnp.where(column == 0, row, R_DEV + row), 255)
    facts = [lane, target, live.astype(jnp.int32), rim_target]
    facts = jnp.concatenate([f.astype(jnp.float32) for f in facts + [lane] * 4], axis=0).astype(jnp.bfloat16)
    moved = dot_nt(facts, move).astype(jnp.int32)
    used = moved[2:3] > 0
    chosen_ref[...] = as_bf16((moved[1:2] == iota((BLK_ROW * R_DEV, slots), 0)) & used)
    rim_ref[...] = as_bf16((moved[3:4] == iota(rim_ref.shape, 0)) & used)
    counts = [jnp.broadcast_to(n.astype(jnp.int32), (1, slots)) for n in (n_rim, n_live)]
    order_ref[...] = jnp.concatenate([moved[:1]] + counts + [moved[:1]] * 5, axis=0)
    copy = pltpu.make_async_copy(order_ref, order_smem, sem)
    copy.start()
    row = first_row() - HALO + iota(cosine_ref.shape, 0)
    cosine_ref[...] = jnp.cos(LAT_START + (row.astype(jnp.float32) + 0.5) * grid_step)
    copy.wait()


def add_terms(chosen, rest):
    total = None
    for _ in range(3):
        part = rest.astype(jnp.bfloat16)
        rest = rest - part.astype(jnp.float32)
        share = dot(chosen, part)
        total = share if total is None else total + share
    return total


def add_blocks(chosen, rest):
    total = add_terms(chosen, rest)
    field = jnp.concatenate([total[j * R_DEV : (j + 1) * R_DEV] for j in range(BLK_ROW)], axis=1)
    return field.astype(jnp.bfloat16)


def order_tiles(xs, perm_ref, recv_ref, channels, first, count):
    slots = perm_ref.shape[0]
    each = slots // recv_ref.shape[0]
    for i, c in enumerate(channels):
        xs[i, first : first + count] = dot(
            perm_ref[first : first + count], recv_ref[:, c * each : (c + 1) * each, :].reshape(slots, 128)
        )


def multiply(xs, eight, terms, first, count, channels=None):
    channels = channels or range(xs.shape[0])
    row = iota((8 * len(channels), 128), 0) % 8
    masks = [as_bf16(row == j) for j in range(8)]
    for g in range(0, count, 8):
        rows = pl.ds(first + g, 8)
        x = jnp.concatenate([xs[c, rows, :] for c in channels], axis=0).astype(jnp.bfloat16)
        spread = jnp.concatenate([x * mask for mask in masks], axis=1)
        got = dot(spread, eight(g))
        for i, c in enumerate(channels):
            terms[c][rows, :] = got[i * 8 : (i + 1) * 8]


def chunks_of(slots, count):
    return jnp.clip((count - HELD + CHUNK - 1) // CHUNK, 0, (slots - HELD) // CHUNK)


def chunk_steps(order, weight_hbm, weight, xs, terms, sems):
    def fetch(k, carry):
        fetch_weights(order, weight_hbm, weight, sems.at[k], HELD + k * CHUNK, CHUNK, k * CHUNK)
        return carry

    def step(k, carry):
        await_weights(weight_hbm, weight, sems.at[k], CHUNK, k * CHUNK)
        eight = lambda g: weight[pl.ds(k * CHUNK + g, 8)].reshape(8 * 128, 128)
        multiply(xs, eight, terms, pl.multiple_of(HELD + k * CHUNK, 8), CHUNK)
        return carry

    return fetch, step


def rim_kernel(
    order, recv_ref, perm_ref, rim_ref, held_ref, weight_hbm, a_ref, b_ref, term_ref,
    weight, xs, sems,
):
    slots = term_ref.shape[1]
    terms = [term_ref.at[w] for w in range(2)]
    half = slots // 2
    chunks = chunks_of(slots, order[1, 0])
    fetch, step = chunk_steps(order, weight_hbm, weight, xs, terms, sems)
    lax.fori_loop(0, chunks, fetch, 0)
    order_tiles(xs, perm_ref, recv_ref, (2, 3), 0, half)

    @pl.when(HELD + chunks * CHUNK > half)
    def _():
        order_tiles(xs, perm_ref, recv_ref, (2, 3), half, half)

    for term in terms:
        term[HELD:slots, :] = jnp.zeros((slots - HELD, 128), jnp.float32)
    multiply(xs, lambda g: held_ref[g : g + 8].reshape(8 * 128, 128), terms, 0, HELD)
    lax.fori_loop(0, chunks, step, 0)
    winds = [add_terms(rim_ref[...], term[...]) for term in terms]
    left = jnp.concatenate([w[:R_DEV] for w in winds], axis=0)
    right = jnp.concatenate([w[R_DEV:] for w in winds], axis=0)
    odd = is_odd("lon")
    a_ref[...] = jnp.where(odd, left, right).astype(jnp.bfloat16)
    b_ref[...] = jnp.where(odd, right, left).astype(jnp.bfloat16)


def rest_kernel(
    after_ref, order, recv_ref, perm_ref, chosen_ref, term_ref, held_ref, weight_hbm,
    wind_ref, others_ref, weight, xs, term, sems,
):
    slots = term_ref.shape[1]
    channels = 2 + others_ref.shape[0]
    terms = [term.at[c - 2] if c in (2, 3) else others_ref.at[c if c < 2 else c - 2] for c in range(channels)]
    last = chunks_of(slots, order[2, 0])
    fetch, step = chunk_steps(order, weight_hbm, weight, xs, terms, sems)

    lax.fori_loop(0, last, fetch, 0)
    order_tiles(xs, perm_ref, recv_ref, range(channels), 0, slots)
    for target in terms:
        target[HELD:slots, :] = jnp.zeros((slots - HELD, 128), jnp.float32)
    for w in range(2):
        term[w, :HELD] = term_ref[w, :HELD]
    eight = lambda g: held_ref[g : g + 8].reshape(8 * 128, 128)
    multiply(xs, eight, terms, 0, HELD, [c for c in range(channels) if c not in (2, 3)])
    lax.fori_loop(0, last, step, 0)
    for w in range(2):
        wind_ref[w] = add_blocks(chosen_ref[...], term[w])


def finish_kernel(after_ref, chosen_ref, others_ref, wind_ref, out_ref):
    for c in range(out_ref.shape[0]):
        if c in (2, 3):
            out_ref[c] = wind_ref[c - 2]
        else:
            out_ref[c] = add_blocks(chosen_ref[...], others_ref[c if c < 2 else c - 2])


def extend_kernel(wind_ref, from_a_ref, from_b_ref, ext_ref, a_ref, b_ref):
    from_a = from_a_ref[...].astype(jnp.float32)
    from_b = from_b_ref[...].astype(jnp.float32)
    odd = is_odd("lon")
    left = jnp.where(odd, from_a, from_b)
    right = jnp.where(odd, from_b, from_a)
    winds = []
    for w in range(2):
        rows = slice(w * R_DEV, (w + 1) * R_DEV)
        winds.append(jnp.concatenate([left[rows], wind_ref[w].astype(jnp.float32), right[rows]], axis=1))
        ext_ref[w] = winds[w]
    pad = jnp.zeros((8 - 2 * HALO, winds[0].shape[1]), jnp.float32)
    first = jnp.concatenate([w[:HALO] for w in winds] + [pad], axis=0)
    last = jnp.concatenate([w[R_DEV - HALO :] for w in winds] + [pad], axis=0)
    odd = is_odd("band")
    a_ref[...] = jnp.where(odd, first, last).astype(jnp.bfloat16)
    b_ref[...] = jnp.where(odd, last, first).astype(jnp.bfloat16)


def smooth(x):
    rows, columns = x.shape
    x = 2.0 * x + (pltpu.roll(x, 1, 0) + pltpu.roll(x, rows - 1, 0))
    x = 2.0 * x + (pltpu.roll(x, 1, 1) + pltpu.roll(x, columns - 1, 1))
    return x * (1.0 / 16.0)


def smooth_kernel(all_rows, cosine_ref, ext_ref, from_a_ref, from_b_ref, out_ref):
    from_a = from_a_ref[...].astype(jnp.float32)
    from_b = from_b_ref[...].astype(jnp.float32)
    odd = is_odd("band")
    above = jnp.where(odd, from_a, from_b)
    below = jnp.where(odd, from_b, from_a)
    pad = jnp.zeros((EXT - R_DEV - 2 * HALO, above.shape[1]), jnp.float32)
    east, north = (
        jnp.concatenate([above[w * HALO : (w + 1) * HALO], ext_ref[w], below[w * HALO : (w + 1) * HALO], pad], axis=0)
        for w in range(2)
    )
    rows, columns = east.shape
    row = first_row() - HALO + iota((rows, 128), 0)
    inside = jnp.tile((row >= 0) & (row < all_rows), (1, columns // 128))
    cosine = cosine_ref[...]
    scaled = east * jnp.tile(cosine, (1, columns // 128))
    half = jnp.tile(0.5 / cosine, (1, columns // 128))
    along = pltpu.roll(north, columns - 1, 1) - pltpu.roll(north, 1, 1)
    across = pltpu.roll(scaled, rows - 1, 0) - pltpu.roll(scaled, 1, 0)
    field = jnp.where(inside, (along - across) * half, 0.0)
    field = jnp.where(inside, smooth(field), 0.0)
    field = smooth(field)
    out_ref[...] = field[HALO : HALO + R_DEV, 128 : 128 + C_DEV]


def call(kernel, outs, ins, scratch=(), vmem=2 << 20, cycles=0, out_specs=None):
    return pl.pallas_call(
        kernel,
        out_shape=outs,
        in_specs=ins,
        out_specs=out_specs or jax.tree.map(lambda _: VM, outs),
        scratch_shapes=scratch,
        compiler_params=pltpu.CompilerParams(vmem_limit_bytes=vmem),
        cost_estimate=pl.CostEstimate(flops=cycles, bytes_accessed=cycles, transcendentals=0) if cycles else None,
    )


def on_device(src_tiles, ent_tile, ent_block, ent_weight, live_count):
    bands, lons = lax.axis_size("band"), lax.axis_size("lon")
    channels, tiles, pixels = src_tiles.shape
    slots = ent_tile.shape[0]
    each = 2 * slots // bands
    shape = jax.ShapeDtypeStruct
    bf16, f32, i32 = jnp.bfloat16, jnp.float32, jnp.int32
    dmas = pltpu.SemaphoreType.DMA
    held = pltpu.with_memory_space_constraint

    chips = bands // 2
    same_core = [[chip * 2 + core for chip in range(chips)] for core in range(2)]
    exchange = lambda x: lax.all_to_all(x, "band", 0, 0, tiled=True, axis_index_groups=same_core)
    pairs_a = lambda size: [(i, i ^ 1) for i in range(size)]
    mate_tiles = lax.ppermute(src_tiles, "band", pairs_a(bands))
    req, pos, own_tiles = call(
        functools.partial(route_kernel, lons * tiles, tiles),
        (shape((chips, 128), i32), shape((8, slots), i32), shape(src_tiles.shape, bf16)),
        [HB, HB],
        [pltpu.VMEM((1, slots), i32), dmas, dmas((2,))],
    )(held(ent_tile.reshape(1, slots), pltpu.HBM), held(src_tiles, pltpu.HBM))
    asked = exchange(req)
    send = call(
        pick_kernel,
        pltpu.HBM((chips, channels * each, pixels), bf16),
        [VM, VM, VM],
        [pltpu.VMEM((channels, chips, each, pixels), bf16), dmas((channels,))],
        out_specs=HB,
    )(asked, held(own_tiles, pltpu.VMEM), held(mate_tiles, pltpu.VMEM))
    perm, chosen, rim, order, cosine = call(
        functools.partial(select_kernel, BLK_ROW * lons, 2.0 * math.pi / (C_DEV * lons)),
        (
            shape((slots, slots), bf16),
            shape((BLK_ROW * R_DEV, slots), bf16),
            shape((2 * R_DEV, slots), bf16),
            pltpu.SMEM((8, slots), i32),
            shape((EXT, 128), f32),
        ),
        [ANY, SM, VM, VM],
        [pltpu.VMEM((8, slots), i32), dmas],
        out_specs=(VM, VM, VM, SM, VM),
        cycles=slots * slots * 8,
    )(held(send, pltpu.HBM), live_count, pos, ent_block.reshape(1, slots))
    order = held(order, pltpu.SMEM)
    weight_hbm = held(ent_weight, pltpu.HBM)
    recv = exchange(send)
    weight_held = call(
        hold_kernel,
        pltpu.VMEM((HELD, pixels, BW), bf16),
        [SM, ANY, HB],
        [dmas((HELD // 8,))],
        cycles=2 * HELD * pixels * BW,
    )(order, held(send, pltpu.HBM), weight_hbm)

    sides, rows = shape((2 * R_DEV, 128), bf16), shape((8, C_DEV + 256), bf16)
    chunks = (slots - HELD) // CHUNK
    weight = pltpu.VMEM((slots - HELD, pixels, BW), bf16)
    per_slot = lambda count: pltpu.VMEM((count, slots, 128), f32)
    weight_held = held(weight_held, pltpu.VMEM)
    to_a, to_b, term = call(
        rim_kernel,
        (sides, sides, shape((2, slots, BW), f32)),
        [SM, VM, VM, VM, VM, HB],
        [weight, per_slot(2), dmas((chunks,))],
        vmem=12 << 20,
    )(order, recv, perm, rim, weight_held, weight_hbm)
    wind, others = call(
        rest_kernel,
        (shape((2, R_DEV, C_DEV), bf16), shape((channels - 2, slots, BW), f32)),
        [ANY, SM, VM, VM, VM, VM, VM, HB],
        [weight, per_slot(channels), per_slot(2), dmas((chunks,))],
        vmem=12 << 20,
        cycles=slots * pixels * BW,
    )(to_b, order, recv, perm, chosen, term, weight_held, weight_hbm)

    pairs_b = [(i, i + 1 if i % 2 else i - 1) for i in range(1, bands - 1)]
    ring_b = [(i, (i + 1 if i % 2 else i - 1) % lons) for i in range(lons)]
    from_a = lax.ppermute(to_a, "lon", pairs_a(lons))
    from_b = lax.ppermute(to_b, "lon", ring_b)
    ext, to_a, to_b = call(extend_kernel, (shape((2, R_DEV, C_DEV + 256), f32), rows, rows), [VM, VM, VM])(
        wind, from_a, from_b
    )
    remapped = call(
        finish_kernel, shape((channels, R_DEV, C_DEV), bf16), [ANY, VM, VM, VM], cycles=slots * slots * 16
    )(to_a, chosen, others, wind)
    from_a = lax.ppermute(to_a, "band", pairs_a(bands))
    from_b = lax.ppermute(to_b, "band", pairs_b)
    smoothed = call(
        functools.partial(smooth_kernel, R_DEV * bands),
        shape((R_DEV, C_DEV), f32),
        [VM, VM, VM, VM],
    )(cosine, ext, from_a, from_b)
    return remapped, smoothed


def solution(mesh):
    in_specs = (
        P(None, ("band", "lon"), None),
        P(("band", "lon")),
        P(("band", "lon")),
        P(("band", "lon"), None, None),
        P(("band", "lon")),
    )
    out_specs = (P(None, "band", "lon"), P("band", "lon"))
    return jax.shard_map(on_device, mesh=mesh, in_specs=in_specs, out_specs=out_specs, check_vma=False)
```

```python
import functools
import math

import jax
import jax.numpy as jnp
from jax import lax
from jax.experimental import pallas as pl
from jax.experimental.pallas import tpu as pltpu
from jax.sharding import PartitionSpec as P

BW = 128
R_DEV = 16
C_DEV = 1024
BLK_ROW = C_DEV // BW
LAT_START = 0.5
HALO = 3
HELD = 88
FIRST = 56
CHUNK = 24
EXT = 24

VM = pl.BlockSpec(memory_space=pltpu.VMEM)
SM = pl.BlockSpec(memory_space=pltpu.SMEM)
HB = pl.BlockSpec(memory_space=pltpu.HBM)
ANY = pl.BlockSpec(memory_space=pl.ANY)


def dot(a, b):
    return jnp.dot(a, b, preferred_element_type=jnp.float32)


def dot_nt(a, b):
    return lax.dot_general(a, b, (((1,), (1,)), ((), ())), preferred_element_type=jnp.float32)


def iota(shape, dim):
    return lax.broadcasted_iota(jnp.int32, shape, dim)


def as_bf16(flags):
    return flags.astype(jnp.float32).astype(jnp.bfloat16)


def is_odd(axis):
    return lax.axis_index(axis) % 2 == 1


def first_row():
    return lax.axis_index("band") * R_DEV


def route_kernel(per_band, tiles_held, tile_hbm, src_hbm, req_ref, pos_ref, src_ref, tile_ref, tile_sem, sems):
    tile_copy = pltpu.make_async_copy(tile_hbm, tile_ref, tile_sem)
    tile_copy.start()
    copies = []
    for h in range(2):
        half = pl.ds(h * (src_ref.shape[0] // 2), src_ref.shape[0] // 2)
        copies.append(pltpu.make_async_copy(src_hbm.at[half], src_ref.at[half], sems.at[h]))
        copies[-1].start()
    tile_copy.wait()
    tile = tile_ref[...]
    slots = tile.shape[1]
    chips = req_ref.shape[0]
    band = tile // per_band
    local = band % 2 * tiles_held + tile % tiles_held
    owner = band // 2
    hit = owner == iota((chips, slots), 0)
    before = as_bf16(iota((slots, slots), 0) < iota((slots, slots), 1))
    earlier = dot(as_bf16(hit), before)
    rank = jnp.sum(jnp.where(hit, earlier, 0.0), axis=0, keepdims=True).astype(jnp.int32)
    place = as_bf16(rank == iota((128, slots), 0))
    high = jnp.where(hit, (local // 16).astype(jnp.float32), 0.0).astype(jnp.bfloat16)
    low = jnp.where(hit, (local % 16).astype(jnp.float32), 0.0).astype(jnp.bfloat16)
    req_ref[...] = (dot_nt(high, place) * 16.0 + dot_nt(low, place)).astype(jnp.int32)
    pos_ref[...] = jnp.broadcast_to(owner * (slots // chips) + rank, (8, slots))
    for copy in copies:
        copy.wait()


def pick_kernel(req_ref, own_ref, mate_ref, send_hbm, picked, sems):
    channels, tiles, _ = own_ref.shape
    _, chips, each, _ = picked.shape
    asked = jnp.transpose(req_ref[...].astype(jnp.float32)).astype(jnp.int32)
    mine = jnp.where(is_odd("band"), tiles, 0)
    cell = iota((each, tiles), 1)
    columns = [jnp.broadcast_to(asked[:each, d : d + 1], (each, tiles)) for d in range(chips)]
    own = jnp.concatenate([as_bf16(column == cell + mine) for column in columns], axis=0)
    mate = jnp.concatenate([as_bf16(column == cell + (tiles - mine)) for column in columns], axis=0)
    copies = []
    for c in range(0, channels, 2):
        pair = lambda ref: jnp.concatenate([ref[c], ref[c + 1]], axis=1)
        got = (dot(own, pair(own_ref)) + dot(mate, pair(mate_ref))).astype(jnp.bfloat16)
        for k in range(2):
            picked[c + k] = got[:, k * 128 : (k + 1) * 128].reshape(chips, each, 128)
            target = send_hbm.at[:, pl.ds((c + k) * each, each)]
            copies.append(pltpu.make_async_copy(picked.at[c + k], target, sems.at[c + k]))
            copies[-1].start()
    for copy in copies:
        copy.wait()


def fetch_weights(order_ref, weight_hbm, target, sem, first, count, offset):
    for i in range(count):
        slot = order_ref[0, first + i]
        pltpu.make_async_copy(weight_hbm.at[slot], target.at[offset + i], sem).start()


def await_weights(weight_hbm, target, sem, count, offset):
    pltpu.make_async_copy(weight_hbm.at[pl.ds(0, count)], target.at[pl.ds(offset, count)], sem).wait()


def hold_kernel(order_ref, after_ref, weight_hbm, held_ref, sems):
    for g in range(sems.shape[0]):
        fetch_weights(order_ref, weight_hbm, held_ref, sems.at[g], g * 8, 8, g * 8)
    for g in range(sems.shape[0]):
        await_weights(weight_hbm, held_ref, sems.at[g], 8, g * 8)


def select_kernel(
    row_stride, grid_step, after_ref, live_ref, pos_ref, block_ref,
    perm_ref, chosen_ref, rim_ref, order_smem, cosine_ref, order_ref, sem,
):
    slots = pos_ref.shape[1]
    block = block_ref[...]
    row, column = (block // row_stride) % R_DEV, block % BLK_ROW
    lane = iota((1, slots), 1)
    live = lane < live_ref[0]
    at_rim = (column == 0) | (column == BLK_ROW - 1)
    kind = jnp.where(live, jnp.where(at_rim, 0, 1), 2)
    kinds = iota((8, slots), 0)
    hit = kind == kinds
    earlier = dot(as_bf16(hit), as_bf16(iota((slots, slots), 0) < iota((slots, slots), 1)))
    n_rim = jnp.sum(jnp.where(kind == 0, 1.0, 0.0), axis=1, keepdims=True)
    n_live = jnp.sum(jnp.where(kind < 2, 1.0, 0.0), axis=1, keepdims=True)
    start = jnp.where(kinds == 1, n_rim, jnp.where(kinds == 2, n_live, 0.0))
    place = jnp.sum(jnp.where(hit, earlier + start, 0.0), axis=0, keepdims=True).astype(jnp.int32)
    move = as_bf16(place == iota((slots, slots), 0))
    where_from = dot_nt(move, pos_ref[...].astype(jnp.float32).astype(jnp.bfloat16))[:, :1].astype(jnp.int32)
    perm_ref[...] = as_bf16(where_from == iota((slots, slots), 1))
    target = column * R_DEV + row
    rim_target = jnp.where(at_rim, jnp.where(column == 0, row, R_DEV + row), 255)
    facts = [lane, target, live.astype(jnp.int32), rim_target]
    facts = jnp.concatenate([f.astype(jnp.float32) for f in facts + [lane] * 4], axis=0).astype(jnp.bfloat16)
    moved = dot_nt(facts, move).astype(jnp.int32)
    used = moved[2:3] > 0
    chosen_ref[...] = as_bf16((moved[1:2] == iota((BLK_ROW * R_DEV, slots), 0)) & used)
    rim_ref[...] = as_bf16((moved[3:4] == iota(rim_ref.shape, 0)) & used)
    counts = [jnp.broadcast_to(n.astype(jnp.int32), (1, slots)) for n in (n_rim, n_live)]
    order_ref[...] = jnp.concatenate([moved[:1]] + counts + [moved[:1]] * 5, axis=0)
    copy = pltpu.make_async_copy(order_ref, order_smem, sem)
    copy.start()
    row = first_row() - HALO + iota(cosine_ref.shape, 0)
    cosine_ref[...] = jnp.cos(LAT_START + (row.astype(jnp.float32) + 0.5) * grid_step)
    copy.wait()


def add_terms(chosen, rest):
    total = None
    for _ in range(3):
        part = rest.astype(jnp.bfloat16)
        rest = rest - part.astype(jnp.float32)
        share = dot(chosen, part)
        total = share if total is None else total + share
    return total


def add_blocks(chosen, rest):
    total = add_terms(chosen, rest)
    field = jnp.concatenate([total[j * R_DEV : (j + 1) * R_DEV] for j in range(BLK_ROW)], axis=1)
    return field.astype(jnp.bfloat16)


def order_tiles(xs, perm_ref, recv_ref, channels, first, count):
    slots = perm_ref.shape[0]
    each = slots // recv_ref.shape[0]
    for i, c in enumerate(channels):
        xs[i, first : first + count] = dot(
            perm_ref[first : first + count], recv_ref[:, c * each : (c + 1) * each, :].reshape(slots, 128)
        )


def multiply(xs, eight, terms, first, count, channels=None):
    channels = channels or range(xs.shape[0])
    row = iota((8 * len(channels), 128), 0) % 8
    masks = [as_bf16(row == j) for j in range(8)]
    for g in range(0, count, 8):
        rows = pl.ds(first + g, 8)
        x = jnp.concatenate([xs[c, rows, :] for c in channels], axis=0).astype(jnp.bfloat16)
        spread = jnp.concatenate([x * mask for mask in masks], axis=1)
        got = dot(spread, eight(g))
        for i, c in enumerate(channels):
            terms[c][rows, :] = got[i * 8 : (i + 1) * 8]


def chunks_of(slots, count):
    return jnp.clip((count - HELD + CHUNK - 1) // CHUNK, 0, (slots - HELD) // CHUNK)


def chunk_steps(order, weight_hbm, weight, xs, terms, sems):
    def fetch(k, carry):
        fetch_weights(order, weight_hbm, weight, sems.at[k], HELD + k * CHUNK, CHUNK, k * CHUNK)
        return carry

    def step(k, carry):
        await_weights(weight_hbm, weight, sems.at[k], CHUNK, k * CHUNK)
        eight = lambda g: weight[pl.ds(k * CHUNK + g, 8)].reshape(8 * 128, 128)
        multiply(xs, eight, terms, pl.multiple_of(HELD + k * CHUNK, 8), CHUNK)
        return carry

    return fetch, step


def rim_kernel(
    order, recv_ref, perm_ref, rim_ref, held_ref, weight_hbm, a_ref, b_ref, term_ref,
    weight, xs, sems,
):
    slots = term_ref.shape[1]
    terms = [term_ref.at[w] for w in range(2)]
    half = slots // 2
    chunks = chunks_of(slots, order[1, 0])
    fetch, step = chunk_steps(order, weight_hbm, weight, xs, terms, sems)
    lax.fori_loop(0, chunks, fetch, 0)
    order_tiles(xs, perm_ref, recv_ref, (2, 3), 0, half)

    @pl.when(HELD + chunks * CHUNK > half)
    def _():
        order_tiles(xs, perm_ref, recv_ref, (2, 3), half, half)

    for term in terms:
        term[FIRST:slots, :] = jnp.zeros((slots - FIRST, 128), jnp.float32)
    multiply(xs, lambda g: held_ref[g : g + 8].reshape(8 * 128, 128), terms, 0, FIRST)

    @pl.when(order[1, 0] > FIRST)
    def _():
        eight = lambda g: held_ref[FIRST + g : FIRST + g + 8].reshape(8 * 128, 128)
        multiply(xs, eight, terms, FIRST, HELD - FIRST)

    lax.fori_loop(0, chunks, step, 0)
    winds = [add_terms(rim_ref[...], term[...]) for term in terms]
    left = jnp.concatenate([w[:R_DEV] for w in winds], axis=0)
    right = jnp.concatenate([w[R_DEV:] for w in winds], axis=0)
    odd = is_odd("lon")
    a_ref[...] = jnp.where(odd, left, right).astype(jnp.bfloat16)
    b_ref[...] = jnp.where(odd, right, left).astype(jnp.bfloat16)


def rest_kernel(
    after_ref, order, recv_ref, perm_ref, chosen_ref, term_ref, held_ref, weight_hbm,
    wind_ref, others_ref, weight, xs, term, sems,
):
    slots = term_ref.shape[1]
    channels = 2 + others_ref.shape[0]
    terms = [term.at[c - 2] if c in (2, 3) else others_ref.at[c if c < 2 else c - 2] for c in range(channels)]
    last = chunks_of(slots, order[2, 0])
    fetch, step = chunk_steps(order, weight_hbm, weight, xs, terms, sems)

    lax.fori_loop(0, last, fetch, 0)
    order_tiles(xs, perm_ref, recv_ref, range(channels), 0, slots)
    for target in terms:
        target[HELD:slots, :] = jnp.zeros((slots - HELD, 128), jnp.float32)
    for w in range(2):
        term[w, :FIRST] = term_ref[w, :FIRST]
    eight = lambda g: held_ref[g : g + 8].reshape(8 * 128, 128)
    multiply(xs, eight, terms, 0, FIRST, [c for c in range(channels) if c not in (2, 3)])
    multiply(xs, lambda g: eight(FIRST + g), terms, FIRST, HELD - FIRST)
    lax.fori_loop(0, last, step, 0)
    for w in range(2):
        wind_ref[w] = add_blocks(chosen_ref[...], term[w])


def finish_kernel(after_ref, chosen_ref, others_ref, wind_ref, out_ref):
    for c in range(out_ref.shape[0]):
        if c in (2, 3):
            out_ref[c] = wind_ref[c - 2]
        else:
            out_ref[c] = add_blocks(chosen_ref[...], others_ref[c if c < 2 else c - 2])


def extend_kernel(wind_ref, from_a_ref, from_b_ref, ext_ref, a_ref, b_ref):
    from_a = from_a_ref[...].astype(jnp.float32)
    from_b = from_b_ref[...].astype(jnp.float32)
    odd = is_odd("lon")
    left = jnp.where(odd, from_a, from_b)
    right = jnp.where(odd, from_b, from_a)
    winds = []
    for w in range(2):
        rows = slice(w * R_DEV, (w + 1) * R_DEV)
        winds.append(jnp.concatenate([left[rows], wind_ref[w].astype(jnp.float32), right[rows]], axis=1))
        ext_ref[w] = winds[w]
    pad = jnp.zeros((8 - 2 * HALO, winds[0].shape[1]), jnp.float32)
    first = jnp.concatenate([w[:HALO] for w in winds] + [pad], axis=0)
    last = jnp.concatenate([w[R_DEV - HALO :] for w in winds] + [pad], axis=0)
    odd = is_odd("band")
    a_ref[...] = jnp.where(odd, first, last).astype(jnp.bfloat16)
    b_ref[...] = jnp.where(odd, last, first).astype(jnp.bfloat16)


def smooth(x):
    rows, columns = x.shape
    x = 2.0 * x + (pltpu.roll(x, 1, 0) + pltpu.roll(x, rows - 1, 0))
    x = 2.0 * x + (pltpu.roll(x, 1, 1) + pltpu.roll(x, columns - 1, 1))
    return x * (1.0 / 16.0)


def smooth_kernel(all_rows, cosine_ref, ext_ref, from_a_ref, from_b_ref, out_ref):
    from_a = from_a_ref[...].astype(jnp.float32)
    from_b = from_b_ref[...].astype(jnp.float32)
    odd = is_odd("band")
    above = jnp.where(odd, from_a, from_b)
    below = jnp.where(odd, from_b, from_a)
    pad = jnp.zeros((EXT - R_DEV - 2 * HALO, above.shape[1]), jnp.float32)
    east, north = (
        jnp.concatenate([above[w * HALO : (w + 1) * HALO], ext_ref[w], below[w * HALO : (w + 1) * HALO], pad], axis=0)
        for w in range(2)
    )
    rows, columns = east.shape
    row = first_row() - HALO + iota((rows, 128), 0)
    inside = jnp.tile((row >= 0) & (row < all_rows), (1, columns // 128))
    cosine = cosine_ref[...]
    scaled = east * jnp.tile(cosine, (1, columns // 128))
    half = jnp.tile(0.5 / cosine, (1, columns // 128))
    along = pltpu.roll(north, columns - 1, 1) - pltpu.roll(north, 1, 1)
    across = pltpu.roll(scaled, rows - 1, 0) - pltpu.roll(scaled, 1, 0)
    field = jnp.where(inside, (along - across) * half, 0.0)
    field = jnp.where(inside, smooth(field), 0.0)
    field = smooth(field)
    out_ref[...] = field[HALO : HALO + R_DEV, 128 : 128 + C_DEV]


def call(kernel, outs, ins, scratch=(), vmem=2 << 20, cycles=0, out_specs=None):
    return pl.pallas_call(
        kernel,
        out_shape=outs,
        in_specs=ins,
        out_specs=out_specs or jax.tree.map(lambda _: VM, outs),
        scratch_shapes=scratch,
        compiler_params=pltpu.CompilerParams(vmem_limit_bytes=vmem),
        cost_estimate=pl.CostEstimate(flops=cycles, bytes_accessed=cycles, transcendentals=0) if cycles else None,
    )


def on_device(src_tiles, ent_tile, ent_block, ent_weight, live_count):
    bands, lons = lax.axis_size("band"), lax.axis_size("lon")
    channels, tiles, pixels = src_tiles.shape
    slots = ent_tile.shape[0]
    each = 2 * slots // bands
    shape = jax.ShapeDtypeStruct
    bf16, f32, i32 = jnp.bfloat16, jnp.float32, jnp.int32
    dmas = pltpu.SemaphoreType.DMA
    held = pltpu.with_memory_space_constraint

    chips = bands // 2
    same_core = [[chip * 2 + core for chip in range(chips)] for core in range(2)]
    exchange = lambda x: lax.all_to_all(x, "band", 0, 0, tiled=True, axis_index_groups=same_core)
    pairs_a = lambda size: [(i, i ^ 1) for i in range(size)]
    mate_tiles = lax.ppermute(src_tiles, "band", pairs_a(bands))
    req, pos, own_tiles = call(
        functools.partial(route_kernel, lons * tiles, tiles),
        (shape((chips, 128), i32), shape((8, slots), i32), shape(src_tiles.shape, bf16)),
        [HB, HB],
        [pltpu.VMEM((1, slots), i32), dmas, dmas((2,))],
    )(held(ent_tile.reshape(1, slots), pltpu.HBM), held(src_tiles, pltpu.HBM))
    asked = exchange(req)
    send = call(
        pick_kernel,
        pltpu.HBM((chips, channels * each, pixels), bf16),
        [VM, VM, VM],
        [pltpu.VMEM((channels, chips, each, pixels), bf16), dmas((channels,))],
        out_specs=HB,
    )(asked, held(own_tiles, pltpu.VMEM), held(mate_tiles, pltpu.VMEM))
    perm, chosen, rim, order, cosine = call(
        functools.partial(select_kernel, BLK_ROW * lons, 2.0 * math.pi / (C_DEV * lons)),
        (
            shape((slots, slots), bf16),
            shape((BLK_ROW * R_DEV, slots), bf16),
            shape((2 * R_DEV, slots), bf16),
            pltpu.SMEM((8, slots), i32),
            shape((EXT, 128), f32),
        ),
        [ANY, SM, VM, VM],
        [pltpu.VMEM((8, slots), i32), dmas],
        out_specs=(VM, VM, VM, SM, VM),
        cycles=slots * slots * 8,
    )(held(send, pltpu.HBM), live_count, pos, ent_block.reshape(1, slots))
    order = held(order, pltpu.SMEM)
    weight_hbm = held(ent_weight, pltpu.HBM)
    recv = exchange(send)
    weight_held = call(
        hold_kernel,
        pltpu.VMEM((HELD, pixels, BW), bf16),
        [SM, ANY, HB],
        [dmas((HELD // 8,))],
        cycles=2 * HELD * pixels * BW,
    )(order, held(send, pltpu.HBM), weight_hbm)

    sides, rows = shape((2 * R_DEV, 128), bf16), shape((8, C_DEV + 256), bf16)
    chunks = (slots - HELD) // CHUNK
    weight = pltpu.VMEM((slots - HELD, pixels, BW), bf16)
    per_slot = lambda count: pltpu.VMEM((count, slots, 128), f32)
    weight_held = held(weight_held, pltpu.VMEM)
    to_a, to_b, term = call(
        rim_kernel,
        (sides, sides, shape((2, slots, BW), f32)),
        [SM, VM, VM, VM, VM, HB],
        [weight, per_slot(2), dmas((chunks,))],
        vmem=12 << 20,
    )(order, recv, perm, rim, weight_held, weight_hbm)
    wind, others = call(
        rest_kernel,
        (shape((2, R_DEV, C_DEV), bf16), shape((channels - 2, slots, BW), f32)),
        [ANY, SM, VM, VM, VM, VM, VM, HB],
        [weight, per_slot(channels), per_slot(2), dmas((chunks,))],
        vmem=12 << 20,
        cycles=slots * pixels * BW,
    )(to_b, order, recv, perm, chosen, term, weight_held, weight_hbm)

    pairs_b = [(i, i + 1 if i % 2 else i - 1) for i in range(1, bands - 1)]
    ring_b = [(i, (i + 1 if i % 2 else i - 1) % lons) for i in range(lons)]
    from_a = lax.ppermute(to_a, "lon", pairs_a(lons))
    from_b = lax.ppermute(to_b, "lon", ring_b)
    ext, to_a, to_b = call(extend_kernel, (shape((2, R_DEV, C_DEV + 256), f32), rows, rows), [VM, VM, VM])(
        wind, from_a, from_b
    )
    remapped = call(
        finish_kernel, shape((channels, R_DEV, C_DEV), bf16), [ANY, VM, VM, VM], cycles=slots * slots * 16
    )(to_a, chosen, others, wind)
    from_a = lax.ppermute(to_a, "band", pairs_a(bands))
    from_b = lax.ppermute(to_b, "band", pairs_b)
    smoothed = call(
        functools.partial(smooth_kernel, R_DEV * bands),
        shape((R_DEV, C_DEV), f32),
        [VM, VM, VM, VM],
    )(cosine, ext, from_a, from_b)
    return remapped, smoothed


def solution(mesh):
    in_specs = (
        P(None, ("band", "lon"), None),
        P(("band", "lon")),
        P(("band", "lon")),
        P(("band", "lon"), None, None),
        P(("band", "lon")),
    )
    out_specs = (P(None, "band", "lon"), P("band", "lon"))
    return jax.shard_map(on_device, mesh=mesh, in_specs=in_specs, out_specs=out_specs, check_vma=False)
```

```python
import functools
import math

import jax
import jax.numpy as jnp
from jax import lax
from jax.experimental import pallas as pl
from jax.experimental.pallas import tpu as pltpu
from jax.sharding import PartitionSpec as P

BW = 128
R_DEV = 16
C_DEV = 1024
BLK_ROW = C_DEV // BW
LAT_START = 0.5
HALO = 3
HELD = 88
FIRST = 56
CHUNK = 24
EXT = 24

VM = pl.BlockSpec(memory_space=pltpu.VMEM)
SM = pl.BlockSpec(memory_space=pltpu.SMEM)
HB = pl.BlockSpec(memory_space=pltpu.HBM)
ANY = pl.BlockSpec(memory_space=pl.ANY)


def dot(a, b):
    return jnp.dot(a, b, preferred_element_type=jnp.float32)


def dot_nt(a, b):
    return lax.dot_general(a, b, (((1,), (1,)), ((), ())), preferred_element_type=jnp.float32)


def iota(shape, dim):
    return lax.broadcasted_iota(jnp.int32, shape, dim)


def as_bf16(flags):
    return flags.astype(jnp.float32).astype(jnp.bfloat16)


def is_odd(axis):
    return lax.axis_index(axis) % 2 == 1


def first_row():
    return lax.axis_index("band") * R_DEV


def route_kernel(per_band, tiles_held, tile_hbm, src_hbm, req_ref, pos_ref, src_ref, tile_ref, tile_sem, sems):
    tile_copy = pltpu.make_async_copy(tile_hbm, tile_ref, tile_sem)
    tile_copy.start()
    copies = []
    for h in range(2):
        half = pl.ds(h * (src_ref.shape[0] // 2), src_ref.shape[0] // 2)
        copies.append(pltpu.make_async_copy(src_hbm.at[half], src_ref.at[half], sems.at[h]))
        copies[-1].start()
    tile_copy.wait()
    tile = tile_ref[...]
    slots = tile.shape[1]
    chips = req_ref.shape[0]
    band = tile // per_band
    local = band % 2 * tiles_held + tile % tiles_held
    owner = band // 2
    hit = owner == iota((chips, slots), 0)
    before = as_bf16(iota((slots, slots), 0) < iota((slots, slots), 1))
    earlier = dot(as_bf16(hit), before)
    rank = jnp.sum(jnp.where(hit, earlier, 0.0), axis=0, keepdims=True).astype(jnp.int32)
    place = as_bf16(rank == iota((128, slots), 0))
    high = jnp.where(hit, (local // 16).astype(jnp.float32), 0.0).astype(jnp.bfloat16)
    low = jnp.where(hit, (local % 16).astype(jnp.float32), 0.0).astype(jnp.bfloat16)
    req_ref[...] = (dot_nt(high, place) * 16.0 + dot_nt(low, place)).astype(jnp.int32)
    pos_ref[...] = jnp.broadcast_to(owner * (slots // chips) + rank, (8, slots))
    for copy in copies:
        copy.wait()


def pick_kernel(req_ref, own_ref, mate_ref, send_hbm, picked, sem):
    channels, tiles, _ = own_ref.shape
    chips, each = picked.shape[0], picked.shape[1] // channels
    asked = jnp.transpose(req_ref[...].astype(jnp.float32)).astype(jnp.int32)
    mine = jnp.where(is_odd("band"), tiles, 0)
    cell = iota((each, tiles), 1)
    columns = [jnp.broadcast_to(asked[:each, d : d + 1], (each, tiles)) for d in range(chips)]
    own = jnp.concatenate([as_bf16(column == cell + mine) for column in columns], axis=0)
    mate = jnp.concatenate([as_bf16(column == cell + (tiles - mine)) for column in columns], axis=0)
    for c in range(0, channels, 2):
        pair = lambda ref: jnp.concatenate([ref[c], ref[c + 1]], axis=1)
        got = (dot(own, pair(own_ref)) + dot(mate, pair(mate_ref))).astype(jnp.bfloat16)
        for k in range(2):
            part = slice((c + k) * each, (c + k + 1) * each)
            picked[:, part] = got[:, k * 128 : (k + 1) * 128].reshape(chips, each, 128)
    copy = pltpu.make_async_copy(picked, send_hbm, sem)
    copy.start()
    copy.wait()


def fetch_weights(order_ref, weight_hbm, target, sem, first, count, offset):
    for i in range(count):
        slot = order_ref[0, first + i]
        pltpu.make_async_copy(weight_hbm.at[slot], target.at[offset + i], sem).start()


def await_weights(weight_hbm, target, sem, count, offset):
    pltpu.make_async_copy(weight_hbm.at[pl.ds(0, count)], target.at[pl.ds(offset, count)], sem).wait()


def hold_kernel(order_ref, after_ref, weight_hbm, held_ref, sems):
    for g in range(sems.shape[0]):
        fetch_weights(order_ref, weight_hbm, held_ref, sems.at[g], g * 8, 8, g * 8)
    for g in range(sems.shape[0]):
        await_weights(weight_hbm, held_ref, sems.at[g], 8, g * 8)


def select_kernel(
    row_stride, grid_step, after_ref, live_ref, pos_ref, block_ref,
    perm_ref, chosen_ref, rim_ref, order_smem, cosine_ref, order_ref, sem,
):
    slots = pos_ref.shape[1]
    block = block_ref[...]
    row, column = (block // row_stride) % R_DEV, block % BLK_ROW
    lane = iota((1, slots), 1)
    live = lane < live_ref[0]
    at_rim = (column == 0) | (column == BLK_ROW - 1)
    kind = jnp.where(live, jnp.where(at_rim, 0, 1), 2)
    kinds = iota((8, slots), 0)
    hit = kind == kinds
    earlier = dot(as_bf16(hit), as_bf16(iota((slots, slots), 0) < iota((slots, slots), 1)))
    n_rim = jnp.sum(jnp.where(kind == 0, 1.0, 0.0), axis=1, keepdims=True)
    n_live = jnp.sum(jnp.where(kind < 2, 1.0, 0.0), axis=1, keepdims=True)
    start = jnp.where(kinds == 1, n_rim, jnp.where(kinds == 2, n_live, 0.0))
    place = jnp.sum(jnp.where(hit, earlier + start, 0.0), axis=0, keepdims=True).astype(jnp.int32)
    move = as_bf16(place == iota((slots, slots), 0))
    where_from = dot_nt(move, pos_ref[...].astype(jnp.float32).astype(jnp.bfloat16))[:, :1].astype(jnp.int32)
    perm_ref[...] = as_bf16(where_from == iota((slots, slots), 1))
    target = column * R_DEV + row
    rim_target = jnp.where(at_rim, jnp.where(column == 0, row, R_DEV + row), 255)
    facts = [lane, target, live.astype(jnp.int32), rim_target]
    facts = jnp.concatenate([f.astype(jnp.float32) for f in facts + [lane] * 4], axis=0).astype(jnp.bfloat16)
    moved = dot_nt(facts, move).astype(jnp.int32)
    used = moved[2:3] > 0
    chosen_ref[...] = as_bf16((moved[1:2] == iota((BLK_ROW * R_DEV, slots), 0)) & used)
    rim_ref[...] = as_bf16((moved[3:4] == iota(rim_ref.shape, 0)) & used)
    counts = [jnp.broadcast_to(n.astype(jnp.int32), (1, slots)) for n in (n_rim, n_live)]
    order_ref[...] = jnp.concatenate([moved[:1]] + counts + [moved[:1]] * 5, axis=0)
    copy = pltpu.make_async_copy(order_ref, order_smem, sem)
    copy.start()
    row = first_row() - HALO + iota(cosine_ref.shape, 0)
    cosine_ref[...] = jnp.cos(LAT_START + (row.astype(jnp.float32) + 0.5) * grid_step)
    copy.wait()


def add_terms(chosen, rest):
    total = None
    for _ in range(3):
        part = rest.astype(jnp.bfloat16)
        rest = rest - part.astype(jnp.float32)
        share = dot(chosen, part)
        total = share if total is None else total + share
    return total


def add_blocks(chosen, rest):
    total = add_terms(chosen, rest)
    field = jnp.concatenate([total[j * R_DEV : (j + 1) * R_DEV] for j in range(BLK_ROW)], axis=1)
    return field.astype(jnp.bfloat16)


def order_tiles(xs, perm_ref, recv_ref, channels, first, count):
    slots = perm_ref.shape[0]
    each = slots // recv_ref.shape[0]
    for i, c in enumerate(channels):
        xs[i, first : first + count] = dot(
            perm_ref[first : first + count], recv_ref[:, c * each : (c + 1) * each, :].reshape(slots, 128)
        )


def multiply(xs, eight, terms, first, count, channels=None):
    channels = channels or range(xs.shape[0])
    row = iota((8 * len(channels), 128), 0) % 8
    masks = [as_bf16(row == j) for j in range(8)]
    for g in range(0, count, 8):
        rows = pl.ds(first + g, 8)
        x = jnp.concatenate([xs[c, rows, :] for c in channels], axis=0).astype(jnp.bfloat16)
        spread = jnp.concatenate([x * mask for mask in masks], axis=1)
        got = dot(spread, eight(g))
        for i, c in enumerate(channels):
            terms[c][rows, :] = got[i * 8 : (i + 1) * 8]


def chunks_of(slots, count):
    return jnp.clip((count - HELD + CHUNK - 1) // CHUNK, 0, (slots - HELD) // CHUNK)


def chunk_steps(order, weight_hbm, weight, xs, terms, sems):
    def fetch(k, carry):
        fetch_weights(order, weight_hbm, weight, sems.at[k], HELD + k * CHUNK, CHUNK, k * CHUNK)
        return carry

    def step(k, carry):
        await_weights(weight_hbm, weight, sems.at[k], CHUNK, k * CHUNK)
        eight = lambda g: weight[pl.ds(k * CHUNK + g, 8)].reshape(8 * 128, 128)
        multiply(xs, eight, terms, pl.multiple_of(HELD + k * CHUNK, 8), CHUNK)
        return carry

    return fetch, step


def rim_kernel(
    order, recv_ref, perm_ref, rim_ref, held_ref, weight_hbm, a_ref, b_ref, term_ref,
    weight, xs, sems,
):
    slots = term_ref.shape[1]
    terms = [term_ref.at[w] for w in range(2)]
    half = slots // 2
    chunks = chunks_of(slots, order[1, 0])
    fetch, step = chunk_steps(order, weight_hbm, weight, xs, terms, sems)
    lax.fori_loop(0, chunks, fetch, 0)
    order_tiles(xs, perm_ref, recv_ref, (2, 3), 0, half)

    @pl.when(HELD + chunks * CHUNK > half)
    def _():
        order_tiles(xs, perm_ref, recv_ref, (2, 3), half, half)

    for term in terms:
        term[FIRST:slots, :] = jnp.zeros((slots - FIRST, 128), jnp.float32)
    multiply(xs, lambda g: held_ref[g : g + 8].reshape(8 * 128, 128), terms, 0, FIRST)

    @pl.when(order[1, 0] > FIRST)
    def _():
        eight = lambda g: held_ref[FIRST + g : FIRST + g + 8].reshape(8 * 128, 128)
        multiply(xs, eight, terms, FIRST, HELD - FIRST)

    lax.fori_loop(0, chunks, step, 0)
    winds = [add_terms(rim_ref[...], term[...]) for term in terms]
    left = jnp.concatenate([w[:R_DEV] for w in winds], axis=0)
    right = jnp.concatenate([w[R_DEV:] for w in winds], axis=0)
    odd = is_odd("lon")
    a_ref[...] = jnp.where(odd, left, right).astype(jnp.bfloat16)
    b_ref[...] = jnp.where(odd, right, left).astype(jnp.bfloat16)


def rest_kernel(
    after_ref, order, recv_ref, perm_ref, chosen_ref, term_ref, held_ref, weight_hbm,
    wind_ref, others_ref, weight, xs, term, sems,
):
    slots = term_ref.shape[1]
    channels = 2 + others_ref.shape[0]
    terms = [term.at[c - 2] if c in (2, 3) else others_ref.at[c if c < 2 else c - 2] for c in range(channels)]
    last = chunks_of(slots, order[2, 0])
    fetch, step = chunk_steps(order, weight_hbm, weight, xs, terms, sems)

    lax.fori_loop(0, last, fetch, 0)
    order_tiles(xs, perm_ref, recv_ref, range(channels), 0, slots)
    for target in terms:
        target[HELD:slots, :] = jnp.zeros((slots - HELD, 128), jnp.float32)
    for w in range(2):
        term[w, :FIRST] = term_ref[w, :FIRST]
    eight = lambda g: held_ref[g : g + 8].reshape(8 * 128, 128)
    multiply(xs, eight, terms, 0, FIRST, [c for c in range(channels) if c not in (2, 3)])
    multiply(xs, lambda g: eight(FIRST + g), terms, FIRST, HELD - FIRST)
    lax.fori_loop(0, last, step, 0)
    for w in range(2):
        wind_ref[w] = add_blocks(chosen_ref[...], term[w])


def spread_lanes(x):
    for _ in range(2):
        x = 2.0 * x + (pltpu.roll(x, 1, 1) + pltpu.roll(x, x.shape[1] - 1, 1))
    return x[:, 128 : 128 + C_DEV]


def difference(x):
    return pltpu.roll(x, x.shape[1] - 1, 1) - pltpu.roll(x, 1, 1)


def finish_kernel(after_ref, chosen_ref, others_ref, wind_ref, ext_ref, out_ref, east_ref, north_ref):
    east_ref[...] = jnp.zeros_like(east_ref)
    north_ref[...] = jnp.zeros_like(north_ref)
    east_ref[HALO : HALO + R_DEV, :] = spread_lanes(ext_ref[0])
    north_ref[HALO : HALO + R_DEV, :] = spread_lanes(difference(ext_ref[1]))
    for c in range(out_ref.shape[0]):
        if c in (2, 3):
            out_ref[c] = wind_ref[c - 2]
        else:
            out_ref[c] = add_blocks(chosen_ref[...], others_ref[c if c < 2 else c - 2])


def extend_kernel(wind_ref, from_a_ref, from_b_ref, ext_ref, a_ref, b_ref):
    from_a = from_a_ref[...].astype(jnp.float32)
    from_b = from_b_ref[...].astype(jnp.float32)
    odd = is_odd("lon")
    left = jnp.where(odd, from_a, from_b)
    right = jnp.where(odd, from_b, from_a)
    winds = []
    for w in range(2):
        rows = slice(w * R_DEV, (w + 1) * R_DEV)
        winds.append(jnp.concatenate([left[rows], wind_ref[w].astype(jnp.float32), right[rows]], axis=1))
        ext_ref[w] = winds[w]
    pad = jnp.zeros((8 - 2 * HALO, winds[0].shape[1]), jnp.float32)
    first = jnp.concatenate([w[:HALO] for w in winds[::-1]] + [pad], axis=0)
    last = jnp.concatenate([w[R_DEV - HALO :] for w in winds] + [pad], axis=0)
    odd = is_odd("band")
    a_ref[...] = jnp.where(odd, first, last).astype(jnp.bfloat16)
    b_ref[...] = jnp.where(odd, last, first).astype(jnp.bfloat16)


def spread_rows(x):
    return 2.0 * x + (pltpu.roll(x, 1, 0) + pltpu.roll(x, x.shape[0] - 1, 0))


def smooth_kernel(all_rows, cosine_ref, east_ref, north_ref, from_a_ref, from_b_ref, out_ref):
    from_a = from_a_ref[...].astype(jnp.float32)
    from_b = from_b_ref[...].astype(jnp.float32)
    odd = is_odd("band")
    above = jnp.where(odd, from_a, from_b)
    below = jnp.where(odd, from_b, from_a)
    top = iota(above.shape, 0) < HALO
    east = spread_lanes(jnp.where(top, above, below))
    north = spread_lanes(difference(jnp.where(top, below, above)))
    top = iota(east.shape, 0) < HALO

    def framed(ref, above, below):
        last = EXT - 8
        return jnp.concatenate(
            [jnp.where(top, above, ref[:8]), ref[8:last], jnp.where(top, ref[last:], below)], axis=0
        )

    east = framed(east_ref, east, east)
    north = framed(north_ref, pltpu.roll(north, 8 - HALO, 0), pltpu.roll(north, HALO, 0))
    rows, columns = east.shape
    row = first_row() - HALO + iota((rows, 128), 0)
    inside = jnp.tile((row >= 0) & (row < all_rows), (1, columns // 128))
    cosine = cosine_ref[...]
    scaled = east * jnp.tile(cosine, (1, columns // 128))
    half = jnp.tile(0.5 / cosine, (1, columns // 128))
    across = pltpu.roll(scaled, rows - 1, 0) - pltpu.roll(scaled, 1, 0)
    field = jnp.where(inside, (north - across) * half, 0.0)
    field = spread_rows(jnp.where(inside, spread_rows(field), 0.0))
    out_ref[...] = field[HALO : HALO + R_DEV] * (1.0 / 256.0)


def call(kernel, outs, ins, scratch=(), vmem=2 << 20, cycles=0, out_specs=None):
    return pl.pallas_call(
        kernel,
        out_shape=outs,
        in_specs=ins,
        out_specs=out_specs or jax.tree.map(lambda _: VM, outs),
        scratch_shapes=scratch,
        compiler_params=pltpu.CompilerParams(vmem_limit_bytes=vmem),
        cost_estimate=pl.CostEstimate(flops=cycles, bytes_accessed=cycles, transcendentals=0) if cycles else None,
    )


def on_device(src_tiles, ent_tile, ent_block, ent_weight, live_count):
    bands, lons = lax.axis_size("band"), lax.axis_size("lon")
    channels, tiles, pixels = src_tiles.shape
    slots = ent_tile.shape[0]
    each = 2 * slots // bands
    shape = jax.ShapeDtypeStruct
    bf16, f32, i32 = jnp.bfloat16, jnp.float32, jnp.int32
    dmas = pltpu.SemaphoreType.DMA
    held = pltpu.with_memory_space_constraint

    chips = bands // 2
    same_core = [[chip * 2 + core for chip in range(chips)] for core in range(2)]
    exchange = lambda x: lax.all_to_all(x, "band", 0, 0, tiled=True, axis_index_groups=same_core)
    pairs_a = lambda size: [(i, i ^ 1) for i in range(size)]
    mate_tiles = lax.ppermute(src_tiles, "band", pairs_a(bands))
    req, pos, own_tiles = call(
        functools.partial(route_kernel, lons * tiles, tiles),
        (shape((chips, 128), i32), shape((8, slots), i32), shape(src_tiles.shape, bf16)),
        [HB, HB],
        [pltpu.VMEM((1, slots), i32), dmas, dmas((2,))],
    )(held(ent_tile.reshape(1, slots), pltpu.HBM), held(src_tiles, pltpu.HBM))
    asked = exchange(req)
    send = call(
        pick_kernel,
        pltpu.HBM((chips, channels * each, pixels), bf16),
        [VM, VM, VM],
        [pltpu.VMEM((chips, channels * each, pixels), bf16), dmas],
        out_specs=HB,
    )(asked, held(own_tiles, pltpu.VMEM), held(mate_tiles, pltpu.VMEM))
    perm, chosen, rim, order, cosine = call(
        functools.partial(select_kernel, BLK_ROW * lons, 2.0 * math.pi / (C_DEV * lons)),
        (
            shape((slots, slots), bf16),
            shape((BLK_ROW * R_DEV, slots), bf16),
            shape((2 * R_DEV, slots), bf16),
            pltpu.SMEM((8, slots), i32),
            shape((EXT, 128), f32),
        ),
        [ANY, SM, VM, VM],
        [pltpu.VMEM((8, slots), i32), dmas],
        out_specs=(VM, VM, VM, SM, VM),
        cycles=slots * slots * 8,
    )(held(send, pltpu.HBM), live_count, pos, ent_block.reshape(1, slots))
    order = held(order, pltpu.SMEM)
    weight_hbm = held(ent_weight, pltpu.HBM)
    recv = exchange(send)
    weight_held = call(
        hold_kernel,
        pltpu.VMEM((HELD, pixels, BW), bf16),
        [SM, ANY, HB],
        [dmas((HELD // 8,))],
        cycles=2 * HELD * pixels * BW,
    )(order, held(send, pltpu.HBM), weight_hbm)

    sides, rows = shape((2 * R_DEV, 128), bf16), shape((8, C_DEV + 256), bf16)
    chunks = (slots - HELD) // CHUNK
    weight = pltpu.VMEM((slots - HELD, pixels, BW), bf16)
    per_slot = lambda count: pltpu.VMEM((count, slots, 128), f32)
    weight_held = held(weight_held, pltpu.VMEM)
    to_a, to_b, term = call(
        rim_kernel,
        (sides, sides, shape((2, slots, BW), f32)),
        [SM, VM, VM, VM, VM, HB],
        [weight, per_slot(2), dmas((chunks,))],
        vmem=12 << 20,
    )(order, recv, perm, rim, weight_held, weight_hbm)
    wind, others = call(
        rest_kernel,
        (shape((2, R_DEV, C_DEV), bf16), shape((channels - 2, slots, BW), f32)),
        [ANY, SM, VM, VM, VM, VM, VM, HB],
        [weight, per_slot(channels), per_slot(2), dmas((chunks,))],
        vmem=12 << 20,
        cycles=slots * pixels * BW,
    )(to_b, order, recv, perm, chosen, term, weight_held, weight_hbm)

    pairs_b = [(i, i + 1 if i % 2 else i - 1) for i in range(1, bands - 1)]
    ring_b = [(i, (i + 1 if i % 2 else i - 1) % lons) for i in range(lons)]
    from_a = lax.ppermute(to_a, "lon", pairs_a(lons))
    from_b = lax.ppermute(to_b, "lon", ring_b)
    ext, to_a, to_b = call(extend_kernel, (shape((2, R_DEV, C_DEV + 256), f32), rows, rows), [VM, VM, VM])(
        wind, from_a, from_b
    )
    remapped, east, north = call(
        finish_kernel,
        (shape((channels, R_DEV, C_DEV), bf16), shape((EXT, C_DEV), f32), shape((EXT, C_DEV), f32)),
        [ANY, VM, VM, VM, VM],
        cycles=slots * slots * 16,
    )(to_a, chosen, others, wind, ext)
    from_a = lax.ppermute(to_a, "band", pairs_a(bands))
    from_b = lax.ppermute(to_b, "band", pairs_b)
    smoothed = call(
        functools.partial(smooth_kernel, R_DEV * bands),
        shape((R_DEV, C_DEV), f32),
        [VM, VM, VM, VM, VM],
    )(cosine, east, north, from_a, from_b)
    return remapped, smoothed


def solution(mesh):
    in_specs = (
        P(None, ("band", "lon"), None),
        P(("band", "lon")),
        P(("band", "lon")),
        P(("band", "lon"), None, None),
        P(("band", "lon")),
    )
    out_specs = (P(None, "band", "lon"), P("band", "lon"))
    return jax.shard_map(on_device, mesh=mesh, in_specs=in_specs, out_specs=out_specs, check_vma=False)
```

```python
import functools
import math

import jax
import jax.numpy as jnp
from jax import lax
from jax.experimental import pallas as pl
from jax.experimental.pallas import tpu as pltpu
from jax.sharding import PartitionSpec as P

BW = 128
R_DEV = 16
C_DEV = 1024
BLK_ROW = C_DEV // BW
LAT_START = 0.5
HALO = 3
HELD = 88
FIRST = 48
CHUNK = 24
EXT = 24

VM = pl.BlockSpec(memory_space=pltpu.VMEM)
SM = pl.BlockSpec(memory_space=pltpu.SMEM)
HB = pl.BlockSpec(memory_space=pltpu.HBM)
ANY = pl.BlockSpec(memory_space=pl.ANY)


def dot(a, b):
    return jnp.dot(a, b, preferred_element_type=jnp.float32)


def dot_nt(a, b):
    return lax.dot_general(a, b, (((1,), (1,)), ((), ())), preferred_element_type=jnp.float32)


def iota(shape, dim):
    return lax.broadcasted_iota(jnp.int32, shape, dim)


def as_bf16(flags):
    return flags.astype(jnp.float32).astype(jnp.bfloat16)


def is_odd(axis):
    return lax.axis_index(axis) % 2 == 1


def first_row():
    return lax.axis_index("band") * R_DEV


def route_kernel(per_band, tiles_held, tile_hbm, src_hbm, req_ref, pos_ref, src_ref, tile_ref, tile_sem, sems):
    tile_copy = pltpu.make_async_copy(tile_hbm, tile_ref, tile_sem)
    tile_copy.start()
    copies = []
    for h in range(2):
        half = pl.ds(h * (src_ref.shape[0] // 2), src_ref.shape[0] // 2)
        copies.append(pltpu.make_async_copy(src_hbm.at[half], src_ref.at[half], sems.at[h]))
        copies[-1].start()
    tile_copy.wait()
    tile = tile_ref[...]
    slots = tile.shape[1]
    chips = req_ref.shape[0]
    band = tile // per_band
    local = band % 2 * tiles_held + tile % tiles_held
    owner = band // 2
    hit = owner == iota((chips, slots), 0)
    before = as_bf16(iota((slots, slots), 0) < iota((slots, slots), 1))
    earlier = dot(as_bf16(hit), before)
    rank = jnp.sum(jnp.where(hit, earlier, 0.0), axis=0, keepdims=True).astype(jnp.int32)
    place = as_bf16(rank == iota((128, slots), 0))
    high = jnp.where(hit, (local // 16).astype(jnp.float32), 0.0).astype(jnp.bfloat16)
    low = jnp.where(hit, (local % 16).astype(jnp.float32), 0.0).astype(jnp.bfloat16)
    req_ref[...] = (dot_nt(high, place) * 16.0 + dot_nt(low, place)).astype(jnp.int32)
    pos_ref[...] = jnp.broadcast_to(owner * (slots // chips) + rank, (8, slots))
    for copy in copies:
        copy.wait()


def pick_kernel(req_ref, own_ref, mate_ref, send_hbm, picked, sem):
    channels, tiles, _ = own_ref.shape
    chips, each = picked.shape[0], picked.shape[1] // channels
    asked = jnp.transpose(req_ref[...].astype(jnp.float32)).astype(jnp.int32)
    mine = jnp.where(is_odd("band"), tiles, 0)
    cell = iota((each, tiles), 1)
    columns = [jnp.broadcast_to(asked[:each, d : d + 1], (each, tiles)) for d in range(chips)]
    own = jnp.concatenate([as_bf16(column == cell + mine) for column in columns], axis=0)
    mate = jnp.concatenate([as_bf16(column == cell + (tiles - mine)) for column in columns], axis=0)
    for c in range(0, channels, 2):
        pair = lambda ref: jnp.concatenate([ref[c], ref[c + 1]], axis=1)
        got = (dot(own, pair(own_ref)) + dot(mate, pair(mate_ref))).astype(jnp.bfloat16)
        for k in range(2):
            part = slice((c + k) * each, (c + k + 1) * each)
            picked[:, part] = got[:, k * 128 : (k + 1) * 128].reshape(chips, each, 128)
    copy = pltpu.make_async_copy(picked, send_hbm, sem)
    copy.start()
    copy.wait()


def fetch_weights(order_ref, weight_hbm, target, sem, first, count, offset):
    for i in range(count):
        slot = order_ref[0, first + i]
        pltpu.make_async_copy(weight_hbm.at[slot], target.at[offset + i], sem).start()


def await_weights(weight_hbm, target, sem, count, offset):
    pltpu.make_async_copy(weight_hbm.at[pl.ds(0, count)], target.at[pl.ds(offset, count)], sem).wait()


def hold_kernel(order_ref, after_ref, weight_hbm, held_ref, sems):
    for g in range(sems.shape[0]):
        fetch_weights(order_ref, weight_hbm, held_ref, sems.at[g], g * 8, 8, g * 8)
    for g in range(sems.shape[0]):
        await_weights(weight_hbm, held_ref, sems.at[g], 8, g * 8)


def select_kernel(
    row_stride, grid_step, after_ref, live_ref, pos_ref, block_ref,
    perm_ref, chosen_ref, rim_ref, order_smem, cosine_ref, order_ref, sem,
):
    slots = pos_ref.shape[1]
    block = block_ref[...]
    row, column = (block // row_stride) % R_DEV, block % BLK_ROW
    lane = iota((1, slots), 1)
    live = lane < live_ref[0]
    at_rim = (column == 0) | (column == BLK_ROW - 1)
    kind = jnp.where(live, jnp.where(at_rim, 0, 1), 2)
    kinds = iota((8, slots), 0)
    hit = kind == kinds
    earlier = dot(as_bf16(hit), as_bf16(iota((slots, slots), 0) < iota((slots, slots), 1)))
    n_rim = jnp.sum(jnp.where(kind == 0, 1.0, 0.0), axis=1, keepdims=True)
    n_live = jnp.sum(jnp.where(kind < 2, 1.0, 0.0), axis=1, keepdims=True)
    start = jnp.where(kinds == 1, n_rim, jnp.where(kinds == 2, n_live, 0.0))
    place = jnp.sum(jnp.where(hit, earlier + start, 0.0), axis=0, keepdims=True).astype(jnp.int32)
    move = as_bf16(place == iota((slots, slots), 0))
    where_from = dot_nt(move, pos_ref[...].astype(jnp.float32).astype(jnp.bfloat16))[:, :1].astype(jnp.int32)
    perm_ref[...] = as_bf16(where_from == iota((slots, slots), 1))
    target = column * R_DEV + row
    rim_target = jnp.where(at_rim, jnp.where(column == 0, row, R_DEV + row), 255)
    facts = [lane, target, live.astype(jnp.int32), rim_target]
    facts = jnp.concatenate([f.astype(jnp.float32) for f in facts + [lane] * 4], axis=0).astype(jnp.bfloat16)
    moved = dot_nt(facts, move).astype(jnp.int32)
    used = moved[2:3] > 0
    chosen_ref[...] = as_bf16((moved[1:2] == iota((BLK_ROW * R_DEV, slots), 0)) & used)
    rim_ref[...] = as_bf16((moved[3:4] == iota(rim_ref.shape, 0)) & used)
    counts = [jnp.broadcast_to(n.astype(jnp.int32), (1, slots)) for n in (n_rim, n_live)]
    order_ref[...] = jnp.concatenate([moved[:1]] + counts + [moved[:1]] * 5, axis=0)
    copy = pltpu.make_async_copy(order_ref, order_smem, sem)
    copy.start()
    row = first_row() - HALO + iota(cosine_ref.shape, 0)
    cosine_ref[...] = jnp.cos(LAT_START + (row.astype(jnp.float32) + 0.5) * grid_step)
    copy.wait()


def add_terms(chosen, rest):
    total = None
    for _ in range(3):
        part = rest.astype(jnp.bfloat16)
        rest = rest - part.astype(jnp.float32)
        share = dot(chosen, part)
        total = share if total is None else total + share
    return total


def add_blocks(chosen, rest):
    total = add_terms(chosen, rest)
    field = jnp.concatenate([total[j * R_DEV : (j + 1) * R_DEV] for j in range(BLK_ROW)], axis=1)
    return field.astype(jnp.bfloat16)


def order_tiles(xs, perm_ref, recv_ref, channels, first, count):
    slots = perm_ref.shape[0]
    each = slots // recv_ref.shape[0]
    for i, c in enumerate(channels):
        xs[i, first : first + count] = dot(
            perm_ref[first : first + count], recv_ref[:, c * each : (c + 1) * each, :].reshape(slots, 128)
        )


def multiply(xs, eight, terms, first, count, channels=None):
    channels = channels or range(xs.shape[0])
    row = iota((8 * len(channels), 128), 0) % 8
    masks = [as_bf16(row == j) for j in range(8)]
    for g in range(0, count, 8):
        rows = pl.ds(first + g, 8)
        x = jnp.concatenate([xs[c, rows, :] for c in channels], axis=0).astype(jnp.bfloat16)
        spread = jnp.concatenate([x * mask for mask in masks], axis=1)
        got = dot(spread, eight(g))
        for i, c in enumerate(channels):
            terms[c][rows, :] = got[i * 8 : (i + 1) * 8]


def chunks_of(slots, count):
    return jnp.clip((count - HELD + CHUNK - 1) // CHUNK, 0, (slots - HELD) // CHUNK)


def chunk_steps(order, weight_hbm, weight, xs, terms, sems):
    def fetch(k, carry):
        fetch_weights(order, weight_hbm, weight, sems.at[k], HELD + k * CHUNK, CHUNK, k * CHUNK)
        return carry

    def step(k, carry):
        await_weights(weight_hbm, weight, sems.at[k], CHUNK, k * CHUNK)
        eight = lambda g: weight[pl.ds(k * CHUNK + g, 8)].reshape(8 * 128, 128)
        multiply(xs, eight, terms, pl.multiple_of(HELD + k * CHUNK, 8), CHUNK)
        return carry

    return fetch, step


def rim_kernel(
    order, recv_ref, perm_ref, rim_ref, held_ref, weight_hbm, a_ref, b_ref, term_ref,
    weight, xs, sems,
):
    slots = term_ref.shape[1]
    terms = [term_ref.at[w] for w in range(2)]
    half = slots // 2
    chunks = chunks_of(slots, order[1, 0])
    fetch, step = chunk_steps(order, weight_hbm, weight, xs, terms, sems)
    lax.fori_loop(0, chunks, fetch, 0)
    order_tiles(xs, perm_ref, recv_ref, (2, 3), 0, half)

    @pl.when(HELD + chunks * CHUNK > half)
    def _():
        order_tiles(xs, perm_ref, recv_ref, (2, 3), half, half)

    for term in terms:
        term[FIRST:slots, :] = jnp.zeros((slots - FIRST, 128), jnp.float32)
    multiply(xs, lambda g: held_ref[g : g + 8].reshape(8 * 128, 128), terms, 0, FIRST)

    @pl.when(order[1, 0] > FIRST)
    def _():
        eight = lambda g: held_ref[FIRST + g : FIRST + g + 8].reshape(8 * 128, 128)
        multiply(xs, eight, terms, FIRST, HELD - FIRST)

    lax.fori_loop(0, chunks, step, 0)
    winds = [add_terms(rim_ref[...], term[...]) for term in terms]
    left = jnp.concatenate([w[:R_DEV] for w in winds], axis=0)
    right = jnp.concatenate([w[R_DEV:] for w in winds], axis=0)
    odd = is_odd("lon")
    a_ref[...] = jnp.where(odd, left, right).astype(jnp.bfloat16)
    b_ref[...] = jnp.where(odd, right, left).astype(jnp.bfloat16)


def rest_kernel(
    after_ref, order, recv_ref, perm_ref, chosen_ref, term_ref, held_ref, weight_hbm,
    wind_ref, others_ref, weight, xs, term, sems,
):
    slots = term_ref.shape[1]
    channels = 2 + others_ref.shape[0]
    terms = [term.at[c - 2] if c in (2, 3) else others_ref.at[c if c < 2 else c - 2] for c in range(channels)]
    last = chunks_of(slots, order[2, 0])
    fetch, step = chunk_steps(order, weight_hbm, weight, xs, terms, sems)

    lax.fori_loop(0, last, fetch, 0)
    order_tiles(xs, perm_ref, recv_ref, range(channels), 0, slots)
    for target in terms:
        target[HELD:slots, :] = jnp.zeros((slots - HELD, 128), jnp.float32)
    for w in range(2):
        term[w, :FIRST] = term_ref[w, :FIRST]
    eight = lambda g: held_ref[g : g + 8].reshape(8 * 128, 128)
    multiply(xs, eight, terms, 0, FIRST, [c for c in range(channels) if c not in (2, 3)])
    multiply(xs, lambda g: eight(FIRST + g), terms, FIRST, HELD - FIRST)
    lax.fori_loop(0, last, step, 0)
    for w in range(2):
        wind_ref[w] = add_blocks(chosen_ref[...], term[w])


def spread_lanes(x):
    for _ in range(2):
        x = 2.0 * x + (pltpu.roll(x, 1, 1) + pltpu.roll(x, x.shape[1] - 1, 1))
    return x[:, 128 : 128 + C_DEV]


def difference(x):
    return pltpu.roll(x, x.shape[1] - 1, 1) - pltpu.roll(x, 1, 1)


def finish_kernel(after_ref, chosen_ref, others_ref, wind_ref, ext_ref, out_ref, east_ref, north_ref):
    east_ref[...] = jnp.zeros_like(east_ref)
    north_ref[...] = jnp.zeros_like(north_ref)
    east_ref[HALO : HALO + R_DEV, :] = spread_lanes(ext_ref[0])
    north_ref[HALO : HALO + R_DEV, :] = spread_lanes(difference(ext_ref[1]))
    for c in range(out_ref.shape[0]):
        if c in (2, 3):
            out_ref[c] = wind_ref[c - 2]
        else:
            out_ref[c] = add_blocks(chosen_ref[...], others_ref[c if c < 2 else c - 2])


def extend_kernel(wind_ref, from_a_ref, from_b_ref, ext_ref, a_ref, b_ref):
    from_a = from_a_ref[...].astype(jnp.float32)
    from_b = from_b_ref[...].astype(jnp.float32)
    odd = is_odd("lon")
    left = jnp.where(odd, from_a, from_b)
    right = jnp.where(odd, from_b, from_a)
    winds = []
    for w in range(2):
        rows = slice(w * R_DEV, (w + 1) * R_DEV)
        winds.append(jnp.concatenate([left[rows], wind_ref[w].astype(jnp.float32), right[rows]], axis=1))
        ext_ref[w] = winds[w]
    pad = jnp.zeros((8 - 2 * HALO, winds[0].shape[1]), jnp.float32)
    first = jnp.concatenate([w[:HALO] for w in winds[::-1]] + [pad], axis=0)
    last = jnp.concatenate([w[R_DEV - HALO :] for w in winds] + [pad], axis=0)
    odd = is_odd("band")
    a_ref[...] = jnp.where(odd, first, last).astype(jnp.bfloat16)
    b_ref[...] = jnp.where(odd, last, first).astype(jnp.bfloat16)


def spread_rows(x):
    return 2.0 * x + (pltpu.roll(x, 1, 0) + pltpu.roll(x, x.shape[0] - 1, 0))


def smooth_kernel(all_rows, cosine_ref, east_ref, north_ref, from_a_ref, from_b_ref, out_ref):
    from_a = from_a_ref[...].astype(jnp.float32)
    from_b = from_b_ref[...].astype(jnp.float32)
    odd = is_odd("band")
    above = jnp.where(odd, from_a, from_b)
    below = jnp.where(odd, from_b, from_a)
    top = iota(above.shape, 0) < HALO
    east = spread_lanes(jnp.where(top, above, below))
    north = spread_lanes(difference(jnp.where(top, below, above)))
    top = iota(east.shape, 0) < HALO

    def framed(ref, above, below):
        last = EXT - 8
        return jnp.concatenate(
            [jnp.where(top, above, ref[:8]), ref[8:last], jnp.where(top, ref[last:], below)], axis=0
        )

    east = framed(east_ref, east, east)
    north = framed(north_ref, pltpu.roll(north, 8 - HALO, 0), pltpu.roll(north, HALO, 0))
    rows, columns = east.shape
    row = first_row() - HALO + iota((rows, 128), 0)
    inside = jnp.tile((row >= 0) & (row < all_rows), (1, columns // 128))
    cosine = cosine_ref[...]
    scaled = east * jnp.tile(cosine, (1, columns // 128))
    half = jnp.tile(0.5 / cosine, (1, columns // 128))
    across = pltpu.roll(scaled, rows - 1, 0) - pltpu.roll(scaled, 1, 0)
    field = jnp.where(inside, (north - across) * half, 0.0)
    field = spread_rows(jnp.where(inside, spread_rows(field), 0.0))
    out_ref[...] = field[HALO : HALO + R_DEV] * (1.0 / 256.0)


def call(kernel, outs, ins, scratch=(), vmem=2 << 20, cycles=0, out_specs=None):
    return pl.pallas_call(
        kernel,
        out_shape=outs,
        in_specs=ins,
        out_specs=out_specs or jax.tree.map(lambda _: VM, outs),
        scratch_shapes=scratch,
        compiler_params=pltpu.CompilerParams(vmem_limit_bytes=vmem),
        cost_estimate=pl.CostEstimate(flops=cycles, bytes_accessed=cycles, transcendentals=0) if cycles else None,
    )


def on_device(src_tiles, ent_tile, ent_block, ent_weight, live_count):
    bands, lons = lax.axis_size("band"), lax.axis_size("lon")
    channels, tiles, pixels = src_tiles.shape
    slots = ent_tile.shape[0]
    each = 2 * slots // bands
    shape = jax.ShapeDtypeStruct
    bf16, f32, i32 = jnp.bfloat16, jnp.float32, jnp.int32
    dmas = pltpu.SemaphoreType.DMA
    held = pltpu.with_memory_space_constraint

    chips = bands // 2
    same_core = [[chip * 2 + core for chip in range(chips)] for core in range(2)]
    exchange = lambda x: lax.all_to_all(x, "band", 0, 0, tiled=True, axis_index_groups=same_core)
    pairs_a = lambda size: [(i, i ^ 1) for i in range(size)]
    mate_tiles = lax.ppermute(src_tiles, "band", pairs_a(bands))
    req, pos, own_tiles = call(
        functools.partial(route_kernel, lons * tiles, tiles),
        (shape((chips, 128), i32), shape((8, slots), i32), shape(src_tiles.shape, bf16)),
        [HB, HB],
        [pltpu.VMEM((1, slots), i32), dmas, dmas((2,))],
    )(held(ent_tile.reshape(1, slots), pltpu.HBM), held(src_tiles, pltpu.HBM))
    asked = exchange(req)
    send = call(
        pick_kernel,
        pltpu.HBM((chips, channels * each, pixels), bf16),
        [VM, VM, VM],
        [pltpu.VMEM((chips, channels * each, pixels), bf16), dmas],
        out_specs=HB,
    )(asked, held(own_tiles, pltpu.VMEM), held(mate_tiles, pltpu.VMEM))
    perm, chosen, rim, order, cosine = call(
        functools.partial(select_kernel, BLK_ROW * lons, 2.0 * math.pi / (C_DEV * lons)),
        (
            shape((slots, slots), bf16),
            shape((BLK_ROW * R_DEV, slots), bf16),
            shape((2 * R_DEV, slots), bf16),
            pltpu.SMEM((8, slots), i32),
            shape((EXT, 128), f32),
        ),
        [ANY, SM, VM, VM],
        [pltpu.VMEM((8, slots), i32), dmas],
        out_specs=(VM, VM, VM, SM, VM),
        cycles=slots * slots * 8,
    )(held(send, pltpu.HBM), live_count, pos, ent_block.reshape(1, slots))
    order = held(order, pltpu.SMEM)
    weight_hbm = held(ent_weight, pltpu.HBM)
    recv = exchange(send)
    weight_held = call(
        hold_kernel,
        pltpu.VMEM((HELD, pixels, BW), bf16),
        [SM, ANY, HB],
        [dmas((HELD // 8,))],
        cycles=2 * HELD * pixels * BW,
    )(order, held(send, pltpu.HBM), weight_hbm)

    sides, rows = shape((2 * R_DEV, 128), bf16), shape((8, C_DEV + 256), bf16)
    chunks = (slots - HELD) // CHUNK
    weight = pltpu.VMEM((slots - HELD, pixels, BW), bf16)
    per_slot = lambda count: pltpu.VMEM((count, slots, 128), f32)
    weight_held = held(weight_held, pltpu.VMEM)
    to_a, to_b, term = call(
        rim_kernel,
        (sides, sides, shape((2, slots, BW), f32)),
        [SM, VM, VM, VM, VM, HB],
        [weight, per_slot(2), dmas((chunks,))],
        vmem=12 << 20,
    )(order, recv, perm, rim, weight_held, weight_hbm)
    wind, others = call(
        rest_kernel,
        (shape((2, R_DEV, C_DEV), bf16), shape((channels - 2, slots, BW), f32)),
        [ANY, SM, VM, VM, VM, VM, VM, HB],
        [weight, per_slot(channels), per_slot(2), dmas((chunks,))],
        vmem=12 << 20,
        cycles=slots * pixels * BW,
    )(to_b, order, recv, perm, chosen, term, weight_held, weight_hbm)

    pairs_b = [(i, i + 1 if i % 2 else i - 1) for i in range(1, bands - 1)]
    ring_b = [(i, (i + 1 if i % 2 else i - 1) % lons) for i in range(lons)]
    from_a = lax.ppermute(to_a, "lon", pairs_a(lons))
    from_b = lax.ppermute(to_b, "lon", ring_b)
    ext, to_a, to_b = call(extend_kernel, (shape((2, R_DEV, C_DEV + 256), f32), rows, rows), [VM, VM, VM])(
        wind, from_a, from_b
    )
    remapped, east, north = call(
        finish_kernel,
        (shape((channels, R_DEV, C_DEV), bf16), shape((EXT, C_DEV), f32), shape((EXT, C_DEV), f32)),
        [ANY, VM, VM, VM, VM],
        cycles=slots * slots * 16,
    )(to_a, chosen, others, wind, ext)
    from_a = lax.ppermute(to_a, "band", pairs_a(bands))
    from_b = lax.ppermute(to_b, "band", pairs_b)
    smoothed = call(
        functools.partial(smooth_kernel, R_DEV * bands),
        shape((R_DEV, C_DEV), f32),
        [VM, VM, VM, VM, VM],
    )(cosine, east, north, from_a, from_b)
    return remapped, smoothed


def solution(mesh):
    in_specs = (
        P(None, ("band", "lon"), None),
        P(("band", "lon")),
        P(("band", "lon")),
        P(("band", "lon"), None, None),
        P(("band", "lon")),
    )
    out_specs = (P(None, "band", "lon"), P("band", "lon"))
    return jax.shard_map(on_device, mesh=mesh, in_specs=in_specs, out_specs=out_specs, check_vma=False)
```
